32 devices in a mesh: parts: 2 (over x), sub: 16 (over z, y, core).
Axes of the slice: x: 2, y: 2, z: 4, core: 2. Of those that a mesh axis runs over, the one named last changes fastest.
Arguments:
- load: float32 [64, 16, 16, 128], P(('parts', 'sub')), parts along dimension 0, may hold values from -140 to 140
- stiff_inv: bfloat16 [64, 2048, 2048], P(('parts', 'sub')), parts along dimension 0, may hold values from -4 to 5, as said below
- face_blocks: bfloat16 [64, 16, 128, 128], P(('parts', 'sub')), parts along dimension 0, may hold values from -8 to 10, as said below
- coupling: float32 [64, 24, 2048], P(('parts', 'sub')), parts along dimension 0, may hold values from -0.6 to 0.6
- coarse_inv: float32 [1024, 512], P(('parts', 'sub')), parts along dimension 0, may hold values from -2 to 2, as said below
- corners: int32 [64, 24], P(('parts', 'sub')), parts along dimension 0, may hold values from 0 to 511
- partner: int32 [64, 16], P(('parts', 'sub')), parts along dimension 0, may hold values from 0 to 511, as said below
Outputs:
- multipliers: float32 [64, 16, 16, 128], P(('parts', 'sub')), parts along dimension 0
- residual: float32 [64, 16, 16, 128], P(('parts', 'sub')), parts along dimension 0
The draws below stay inside these ranges and needn't reach their ends.
There are 2 independent parts, one for each index of `parts`. The reference program is written for one: setup_inputs(seed, part) draws one part's arguments, and reference() takes and returns one part's arrays. A program takes and returns all parts, laid end to end along the dimension named above; each array names one. Nothing has to cross between parts.
Inputs may be any that keep to these rules, and one draw needn't show every extreme that they name: `stiff_inv`: every subdomain's matrix is symmetric positive definite. `face_blocks`: every face block is symmetric positive definite. `coarse_inv`: symmetric positive definite. partner[s, j] is the number s2 * 16 + j2 of the face that shares its unknowns, in the same order, with face j of subdomain s; the relation is symmetric; a device of sub holds 2 subdomains in a row; the two faces of a pair lie on devices one, two or three indices apart along sub; between two devices at most 12 pairs of faces are shared, a bound that is reached by some pair of devices at each of the three distances.
All inputs are finite; a program needn't handle non-finite values.
Results may differ from the reference program's by a relative error of at most 0.004.
Values sent between devices are 32-bit elements; how exact they have to be, the bound alone decides.
No kernel may reach another device: no remote copies, remote signals or barrier semaphores. Data moves between devices by JAX's collectives and lax.ppermute only.
A program may use at most 128 MiB of HBM per device.

```python
import math
import jax
import jax.numpy as jnp
import numpy as np
from jax import lax

FACE_DOF = 128
NFACE = 16
F = 2048
SUB_DEV = 2
S = 32
LOADS = 16
NCS = 24
NCOARSE = 512
ITERS = 3


left_design = ((0, 1, 6), (0, 2, 4), (0, 3, 6), (1, 2, 5), (1, 3, 3), (2, 3, 2))


right_design = ((0, 1, 6), (0, 2, 6), (0, 3, 4), (1, 2, 3), (1, 3, 5), (2, 3, 2))


def flip_last(values):
    order = tuple(range(values.ndim - 2)) + (values.ndim - 1, values.ndim - 2)
    return jnp.transpose(values, order)


def draw_load(key, part):
    key = jax.random.fold_in(key, 11)
    key_base = jax.random.fold_in(key, 0)
    position = jnp.arange(S, dtype=jnp.float32) / max(S - 1, 1)
    shape_all = (S, NFACE, LOADS, FACE_DOF)
    rise_factor = jnp.exp(position * math.log(3.0))[:, None, None, None]
    values = jax.random.truncated_normal(key_base, -4.0, 4.0, shape_all, jnp.float32) * rise_factor
    return values


def gram_matrix(entries, unit_scale, diagonal_add):
    width = entries.shape[-2]
    inner_width = entries.shape[-1]
    gram = jnp.matmul(entries, flip_last(entries), precision=lax.Precision.HIGHEST) / inner_width
    core_matrix = gram + diagonal_add * jnp.eye(width, dtype=jnp.float32)
    return unit_scale * flip_last(unit_scale) * core_matrix


def draw_stiff_inv(key, part):
    key = jax.random.fold_in(key, 7)
    key_entries, key_scale = jax.random.split(key)
    inner_width = F // 2
    block_keys = jax.random.split(key_entries, S)
    unit_scale = jnp.exp(jax.random.uniform(key_scale, (S, F, 1), jnp.float32, math.log(0.25), math.log(0.9)))

    def build_block(paired):
        block_key, scale_col = paired
        entries = jax.random.truncated_normal(block_key, -2.0, 2.0, (F, inner_width), jnp.float32)
        return gram_matrix(entries, scale_col, 0.5).astype(jnp.bfloat16)
    return lax.map(build_block, (block_keys, unit_scale))


def draw_face_blocks(key, part):
    key = jax.random.fold_in(key, 13)
    key_entries, key_scale = jax.random.split(key)
    shape_all = (S, NFACE, FACE_DOF, FACE_DOF)
    entries = jax.random.truncated_normal(key_entries, -2.0, 2.0, shape_all, jnp.float32)
    unit_scale = jnp.exp(jax.random.uniform(key_scale, (S, NFACE, FACE_DOF, 1), jnp.float32, math.log(0.6), math.log(1.4)))
    return gram_matrix(entries, unit_scale, 1.0).astype(jnp.bfloat16)


def draw_coarse_inv(key, part):
    key = jax.random.fold_in(key, 17)
    key_entries, key_scale = jax.random.split(key)
    inner_width = NCOARSE // 2
    entries = jax.random.truncated_normal(key_entries, -2.0, 2.0, (NCOARSE, inner_width), jnp.float32)
    unit_scale = jnp.exp(jax.random.uniform(key_scale, (NCOARSE, 1), jnp.float32, math.log(0.5), math.log(1.5)))
    return 0.1 * gram_matrix(entries, unit_scale, 2.0)


def band_table(device_count, scale_unit):
    table = np.zeros((device_count, device_count), np.int32)
    device_ids = np.arange(device_count)
    even_ids = device_ids[0::2]
    table[even_ids, even_ids + 1] = 6 * scale_unit
    table[device_ids[:-2], device_ids[:-2] + 2] = 3 * scale_unit
    table[device_ids[:-3], device_ids[:-3] + 3] = 2 * scale_unit
    table[:4, :4] = 0
    table[device_count - 4:, device_count - 4:] = 0
    for first_dev, second_dev, weight in left_design:
        table[first_dev, second_dev] = weight * scale_unit
    for first_dev, second_dev, weight in right_design:
        table[device_count - 1 - second_dev, device_count - 1 - first_dev] = weight * scale_unit
    return table + table.T


def twist_cycles(device_count):
    chosen = list(range(2, device_count // 2 - 3))
    cycles = np.zeros((max(len(chosen), 1), device_count, device_count), np.int32)
    for position, block_pos in enumerate(chosen):
        first_dev = 2 * block_pos
        cycles[position, first_dev, first_dev + 2] = 1
        cycles[position, first_dev + 1, first_dev + 3] = 1
        cycles[position, first_dev, first_dev + 1] = -1
        cycles[position, first_dev + 2, first_dev + 3] = -1
    return cycles + np.transpose(cycles, (0, 2, 1))


def draw_partner(key, part):
    key = jax.random.fold_in(key, 5)
    key_twist, key_layout = jax.random.split(key)
    face_count = SUB_DEV * NFACE
    device_count = S // SUB_DEV
    scale_unit = face_count // 16
    cycles = twist_cycles(device_count)
    twists = jax.random.randint(key_twist, (cycles.shape[0],), 0, scale_unit + 1, dtype=jnp.int32)
    counts = jnp.asarray(band_table(device_count, scale_unit)) + jnp.tensordot(twists, jnp.asarray(cycles), axes=1).astype(jnp.int32)
    bound_high = jnp.cumsum(counts, axis=1).astype(jnp.int32)
    bound_low = bound_high - counts
    slot_ids = jnp.arange(face_count, dtype=jnp.int32)
    peer_dev = jnp.sum((bound_high[:, None, :] <= slot_ids[None, :, None]).astype(jnp.int32), axis=2).astype(jnp.int32)
    owners = jnp.arange(device_count, dtype=jnp.int32)[:, None]
    rank_pos = slot_ids[None, :] - jnp.take_along_axis(bound_low, peer_dev, axis=1)
    mirror_slot = bound_low[peer_dev, owners] + rank_pos
    layouts = jax.vmap(lambda sub_key: jax.random.permutation(sub_key, face_count))(jax.random.split(key_layout, device_count)).astype(jnp.int32)
    partner_face = peer_dev * face_count + layouts[peer_dev, mirror_slot]
    partner_table = jnp.zeros((device_count, face_count), jnp.int32).at[owners, layouts].set(partner_face)
    return partner_table.reshape(S, NFACE)


def set_ends(array, rng, least, largest):
    longest = array.shape.index(max(array.shape))
    spots = []
    for shift in (0, 1):
        where = [jax.random.randint(jax.random.fold_in(rng, axis), (), 0, length) for axis, length in enumerate(array.shape)]
        where[longest] = (where[longest] + shift) % array.shape[longest]
        spots.append(tuple(where))
    return array.at[spots[0]].set(least).at[spots[1]].set(largest)


def block_levels(rng, extent, cuts, smallest, top_value):
    def one(dim, blocks):
        heights = jax.random.uniform(jax.random.fold_in(jax.random.fold_in(rng, 6), dim), (blocks,), jnp.float32, smallest / len(cuts), top_value / len(cuts))
        return jnp.repeat(jnp.exp(heights), extent[dim] // blocks).reshape((-1,) + (1,) * (len(extent) - dim - 1))

    loudness = one(*cuts[0])
    for cut in cuts[1:]:
        loudness = loudness * one(*cut)
    return loudness


def bell_draw(stream_key, shape, scale, bound, pieces=(), kind=jnp.bfloat16):
    values = scale * jax.random.normal(stream_key, shape, jnp.float32)
    if pieces:
        values = values * block_levels(stream_key, shape, pieces, -0.22, 0.18)
    return jnp.clip(values, -bound, bound).astype(kind)


def setup_inputs(seed: int = 0, part: int = 0) -> dict:
    key_list = jax.random.split(jax.random.key(seed), 8)
    part_keys = jax.random.split(jax.random.fold_in(key_list[7], part), 8)
    return {
        "load": draw_load(jax.random.fold_in(jax.random.fold_in(key_list[7], part), 71), part),
        "stiff_inv": draw_stiff_inv(jax.random.fold_in(jax.random.fold_in(key_list[7], part), 71), part),
        "face_blocks": draw_face_blocks(jax.random.fold_in(jax.random.fold_in(key_list[7], part), 71), part),
        "coupling": bell_draw(part_keys[3], (S, NCS, F), 0.1, 0.6, ((0, 16),), jnp.float32),
        "coarse_inv": draw_coarse_inv(jax.random.fold_in(jax.random.fold_in(key_list[7], part), 71), part),
        "corners": set_ends(jax.random.randint(part_keys[5], (S, NCS), 0, NCOARSE), jax.random.fold_in(part_keys[5], 1), 0, NCOARSE - 1).astype(jnp.int32),
        "partner": draw_partner(jax.random.fold_in(jax.random.fold_in(key_list[7], part), 71), part),
    }


def jump_field(field_vec, partner):
    flat_faces = field_vec.reshape((-1,) + field_vec.shape[2:])
    other_faces = flat_faces[partner.reshape(-1)]
    return field_vec - other_faces.reshape(field_vec.shape)


def local_apply(stiff_inv, vector):
    def per_sub(paired):
        matrix, block_vec = paired
        flat_rows = jnp.transpose(block_vec, (1, 0, 2)).reshape(block_vec.shape[1], -1).astype(jnp.bfloat16)
        product = jnp.dot(flat_rows, matrix, preferred_element_type=jnp.float32)
        product = product.reshape(block_vec.shape[1], block_vec.shape[0], block_vec.shape[2])
        return jnp.transpose(product, (1, 0, 2))
    return lax.map(per_sub, (stiff_inv, vector))


def coarse_apply(coupling, coarse_inv, corners, vector):
    coupling_faces = coupling.reshape(coupling.shape[0], coupling.shape[1], NFACE, FACE_DOF)
    primal_rows = jnp.einsum("scfb,sflb->scl", coupling_faces, vector, precision=lax.Precision.HIGHEST)
    assembled = jnp.zeros((NCOARSE, LOADS), jnp.float32).at[corners.reshape(-1)].add(primal_rows.reshape(-1, LOADS))
    lifted = jnp.dot(assembled.T, coarse_inv, precision=lax.Precision.HIGHEST, preferred_element_type=jnp.float32)
    picked = jnp.transpose(lifted[:, corners], (1, 2, 0))
    return jnp.einsum("scfb,scl->sflb", coupling_faces, picked, precision=lax.Precision.HIGHEST)


def inner_sum(first_vec, second_vec):
    return jnp.sum(first_vec * second_vec, axis=(0, 1, 3))


def reference(load, stiff_inv, face_blocks, coupling, coarse_inv, corners, partner):
    def apply_op(vector):
        return local_apply(stiff_inv, vector) + coarse_apply(coupling, coarse_inv, corners, vector)

    def precond(vector):
        rounded = lax.optimization_barrier(vector.astype(jnp.bfloat16))
        weighted = jnp.einsum("sflb,sfba->sfla", rounded.astype(jnp.float32), face_blocks.astype(jnp.float32), precision=lax.Precision.HIGHEST)
        return 0.25 * jump_field(weighted, partner)

    rhs = jump_field(apply_op(load), partner)
    multipliers = jnp.zeros_like(rhs)
    residual = rhs
    precon_res = precond(residual)
    gamma_now = inner_sum(residual, precon_res)
    direction = precon_res
    for iteration in range(ITERS):
        image_vec = jump_field(apply_op(direction), partner)
        step_size = (gamma_now / inner_sum(direction, image_vec))[None, None, :, None]
        multipliers = multipliers + step_size * direction
        residual = residual - step_size * image_vec
        if iteration + 1 < ITERS:
            precon_res = precond(residual)
            gamma_new = inner_sum(residual, precon_res)
            direction = precon_res + (gamma_new / gamma_now)[None, None, :, None] * direction
            gamma_now = gamma_new
    return multipliers, residual
```

```python
import functools
import jax
import jax.numpy as jnp
from jax import lax
from jax.experimental import pallas as pl
from jax.experimental.pallas import tpu as pltpu
from jax.sharding import PartitionSpec as P

ITERS = 3
LANES = 6
PAD = 32
WIDE = 128
BF = jnp.bfloat16
F32 = jnp.float32
VMEM = pl.BlockSpec(memory_space=pltpu.VMEM)
SMEM = pl.BlockSpec(memory_space=pltpu.SMEM)
HBM = pl.BlockSpec(memory_space=pl.ANY)


def completed(pairs, devices):
    table = dict(pairs)
    table.update({second: first for first, second in pairs})
    free = [i for i in range(devices) if i not in table]
    for first, second in zip(free[0::2], free[1::2]):
        table[first] = second
        table[second] = first
    return sorted(table.items())


def flipped(mask, devices):
    return [(i, i ^ mask) for i in range(devices)]


def lane_pairs(devices):
    odd = range(2, devices - 2, 4)
    return (
        flipped(1, devices),
        flipped(2, devices),
        flipped(3, devices),
        completed([(i + core, i + 2 + core) for i in odd for core in (0, 1)], devices),
        completed([(i + core, i + 3 - core) for i in odd for core in (0, 1)], devices),
        completed([(i, i + 3) for i in range(1, devices - 3, 2)], devices),
    )


def split_hi_lo(value):
    high = value.astype(BF)
    return high, (value - high.astype(F32)).astype(BF)


def routing(partner, capacity):
    face_count = partner.size
    subs = partner.shape[0]
    own = lax.axis_index("sub")
    ids = partner.reshape(face_count)
    peer = ids // face_count
    chip_gap = jnp.abs(peer // 2 - own // 2)
    lowest = jnp.minimum(peer // 2, own // 2)
    crossed = (peer + own) % 2
    lane = jnp.where(chip_gap == 0, 0, jnp.where(chip_gap == 1, 1 + 2 * (lowest % 2) + crossed, 5))
    order = jnp.arange(face_count, dtype=jnp.int32)
    same = lane[:, None] == lane[None, :]
    send_pos = jnp.sum(same & (order[None, :] < order[:, None]), axis=1, dtype=jnp.int32)
    recv_pos = jnp.sum(same & (ids[None, :] < ids[:, None]), axis=1, dtype=jnp.int32)
    slots = jnp.arange(LANES * capacity, dtype=jnp.int32)
    hit = slots[:, None] == (lane * capacity + send_pos)[None, :]
    source = jnp.sum(jnp.where(hit, order[None, :], 0), axis=1, dtype=jnp.int32)
    arrival = lane * capacity + recv_pos
    block = (1 + lane) * subs + (ids // partner.shape[1]) % subs
    return jnp.concatenate([source, arrival, block]).astype(jnp.int32)


class Sizes:
    def __init__(self, load, coupling, coarse_inv):
        self.subs, self.faces, self.loads, self.dof = load.shape
        self.total = self.subs * self.faces
        self.unknowns = self.faces * self.dof
        self.slots_per_lane = 3 * self.total // 8
        self.slots = LANES * self.slots_per_lane
        self.primal = coupling.shape[1]
        self.coarse = coarse_inv.shape[1]
        self.blocks = (1 + LANES) * self.subs
        self.pick_width = -(-self.blocks * PAD // WIDE) * WIDE
        self.carry_rows = self.slots_per_lane * self.primal + 8
        self.small_width = self.coarse + WIDE


def call(kernel, sizes, outs, ins, specs, scratch, limit, name, flops=0, moved=0):
    return pl.pallas_call(
        functools.partial(kernel, sizes),
        out_shape=outs,
        in_specs=specs,
        out_specs=[VMEM] * len(outs),
        scratch_shapes=scratch,
        compiler_params=pltpu.CompilerParams(vmem_limit_bytes=limit * 2**20),
        cost_estimate=pl.CostEstimate(flops=flops, bytes_accessed=moved, transcendentals=0),
        name=name,
    )(*ins)


def shape(*dims, dtype=F32):
    return jax.ShapeDtypeStruct(dims, dtype)


def pack_kernel(z, tab, coupling, corner_row, *rest):
    lanes, weights = rest[:LANES], rest[LANES]
    for lane in range(LANES):
        for pos in range(z.slots_per_lane):
            face = tab[lane * z.slots_per_lane + pos]
            sub = face // z.faces
            start = pl.multiple_of((face - sub * z.faces) * z.dof, z.dof)
            lanes[lane][pos * z.primal:(pos + 1) * z.primal, :] = coupling[sub, :, pl.ds(start, z.dof)]
        lanes[lane][z.slots_per_lane * z.primal:, :] = corner_row[...]
    weights[...] = jnp.zeros_like(weights)
    gap = jnp.zeros((PAD - z.primal, z.unknowns), F32)
    for sub in range(z.subs):
        high, low = split_hi_lo(jnp.concatenate([coupling[sub], gap], axis=0))
        weights[sub, sub * 2 * PAD:sub * 2 * PAD + PAD, :] = high
        weights[sub, sub * 2 * PAD + PAD:sub * 2 * PAD + 2 * PAD, :] = low


def unpack_kernel(z, tab, coupling, corner_row, *rest):
    arrived, rest = rest[:LANES], rest[LANES:]
    spread, pick, held, names = rest
    per = z.slots_per_lane
    width = z.subs * PAD
    names[...] = jnp.full(names.shape, -1.0, F32)
    names[:, 0:width] = corner_row[:, 0:width]
    for lane in range(LANES):
        names[:, (1 + lane) * width:(2 + lane) * width] = arrived[lane][per * z.primal:, 0:width]
        for pos in range(per):
            held[lane * per + pos] = arrived[lane][pos * z.primal:(pos + 1) * z.primal, :]
    rows = lax.broadcasted_iota(jnp.int32, pick.shape, 0).astype(F32)
    pick[...] = jnp.where(rows == names[0:1, :], 1.0, 0.0).astype(BF)
    gap = jnp.zeros((PAD - z.primal, z.dof), F32)
    blank = jnp.zeros((PAD, z.dof), BF)
    for face in range(z.total):
        sub, side = face // z.faces, face % z.faces
        own = coupling[sub, :, side * z.dof:(side + 1) * z.dof]
        other = -held[tab[z.slots + face]]
        for place, value in enumerate((own, other)):
            high, low = split_hi_lo(jnp.concatenate([value, gap], axis=0))
            spread[face, place * 4 * PAD:(place + 1) * 4 * PAD, :] = jnp.concatenate([high, low, high, blank], axis=0)


def stiff_copies(z, stiff, buffer, sems):
    step = z.unknowns // 8
    return [
        pltpu.make_async_copy(
            stiff.at[sub, pl.ds(part * step, step), :],
            buffer.at[sub, pl.ds(part * step, step), :],
            sems.at[sub * 8 + part],
        )
        for sub in range(z.subs)
        for part in range(8)
    ]


def apply_in_kernel(z, tab, vec, gamma, eta, weights, spot, copies, buffer, packed, image, small, lanes):
    for face in range(z.total):
        sub, side = face // z.faces, face % z.faces
        high, low = split_hi_lo(vec[face])
        packed[sub, 0:z.loads, side * z.dof:(side + 1) * z.dof] = high
        packed[sub, z.loads:, side * z.dof:(side + 1) * z.dof] = low
    rows = None
    for sub in range(z.subs):
        part = lax.dot_general(
            packed[sub], weights[sub], (((1,), (1,)), ((), ())), preferred_element_type=F32
        )
        rows = part if rows is None else rows + part
    high, low = split_hi_lo(rows)
    summed = jnp.dot(jnp.concatenate([high, low], axis=0), spot[...], preferred_element_type=F32)
    n = z.loads
    small[:, 0:z.coarse] = (summed[0:n] + summed[n:2 * n]) + (summed[2 * n:3 * n] + summed[3 * n:])
    step = z.unknowns // 8
    kappa = jnp.zeros((z.loads, z.dof), F32)
    for sub in range(z.subs):
        total = jnp.zeros((2 * z.loads, z.unknowns), F32)
        for part in range(8):
            copies[sub * 8 + part].wait()
            total = total + jnp.dot(
                packed[sub, :, part * step:(part + 1) * step],
                buffer[sub, part * step:(part + 1) * step, :],
                preferred_element_type=F32,
            )
        total = total[0:n] + total[n:]
        for side in range(z.faces):
            piece = total[:, side * z.dof:(side + 1) * z.dof]
            image[sub * z.faces + side] = piece
            kappa = kappa + piece * vec[sub * z.faces + side]
    column = lax.broadcasted_iota(jnp.int32, (z.loads, WIDE), 1)
    tail = jnp.where(column == 1, jnp.sum(kappa, axis=1, keepdims=True), 0.0)
    if gamma is not None:
        tail = jnp.where(column == 0, jnp.sum(gamma, axis=1, keepdims=True), tail)
        tail = jnp.where(column == 2, jnp.sum(eta, axis=1, keepdims=True), tail)
    small[:, z.coarse:] = tail
    fill_lanes(z, tab, image, lanes)


def fill_lanes(z, tab, field, lanes):
    for lane in range(LANES):
        for pos in range(z.slots_per_lane):
            lanes[lane][pos] = field[tab[lane * z.slots_per_lane + pos]]


def take_lanes(z, arrived, held):
    per = z.slots_per_lane
    for lane in range(LANES):
        held[lane * per:(lane + 1) * per] = arrived[lane][...]


def load_kernel(z, tab, load, weights, spot, stiff, image, small, *rest):
    lanes, (buffer, packed, sems) = rest[:LANES], rest[LANES:]
    copies = stiff_copies(z, stiff, buffer, sems)
    for copy in copies:
        copy.start()
    apply_in_kernel(z, tab, load, None, None, weights, spot, copies, buffer, packed, image, small, lanes)


def precond_kernel(z, tab, weighted, residual, old_image, weights, spot, stiff, *rest):
    arrived, rest = rest[:LANES], rest[LANES:]
    vec, image, small = rest[:3]
    lanes, (buffer, packed, sems, held) = rest[3:3 + LANES], rest[3 + LANES:]
    copies = stiff_copies(z, stiff, buffer, sems)
    for copy in copies:
        copy.start()
    take_lanes(z, arrived, held)
    gamma = jnp.zeros((z.loads, z.dof), F32)
    eta = jnp.zeros((z.loads, z.dof), F32)
    for face in range(z.total):
        value = 0.25 * (weighted[face] - held[tab[z.slots + face]])
        vec[face] = value
        gamma = gamma + residual[face] * value
        eta = eta + old_image[face] * value
    apply_in_kernel(z, tab, vec, gamma, eta, weights, spot, copies, buffer, packed, image, small, lanes)


def coarse_in_kernel(z, small, coarse, pick, picked):
    n = z.loads
    primal = small[:, 0:z.coarse]
    high, low = split_hi_lo(primal)
    inv_high, inv_low = split_hi_lo(coarse[...])
    both = jnp.dot(jnp.concatenate([high, low], axis=0), inv_high, preferred_element_type=F32)
    lifted = (both[0:n] + both[n:]) + jnp.dot(high, inv_low, preferred_element_type=F32)
    energy = jnp.sum(primal * lifted, axis=1, keepdims=True)
    high, low = split_hi_lo(lifted)
    values = jnp.dot(jnp.concatenate([high, low], axis=0), pick[...], preferred_element_type=F32)
    column = lax.broadcasted_iota(jnp.int32, (n, WIDE), 1)
    for block in range(z.blocks):
        group, place = divmod(block * PAD, WIDE)
        upper = values[0:n, group * WIDE:(group + 1) * WIDE]
        lower = values[n:, group * WIDE:(group + 1) * WIDE]
        first = pltpu.roll(upper, (WIDE - place) % WIDE, 1)
        second = pltpu.roll(upper, (WIDE + PAD - place) % WIDE, 1)
        third = pltpu.roll(lower, (WIDE + 2 * PAD - place) % WIDE, 1)
        mixed = jnp.where(column < PAD, first, jnp.where(column < 2 * PAD, second, third))
        picked[block] = jnp.where(column < 3 * PAD, mixed, 0.0).astype(BF)
    return energy


def image_of_face(z, tab, face, image, held, picked, spread):
    sides = jnp.concatenate([picked[face // z.faces], picked[tab[z.slots + z.total + face]]], axis=1)
    lift = jnp.dot(sides, spread[face], preferred_element_type=F32)
    return (image[face] - held[tab[z.slots + face]]) + lift


def start_kernel(z, tab, image, small_a, small_b, coarse, pick, spread, blocks, *rest):
    arrived, rest = rest[:LANES], rest[LANES:]
    residual, weighted = rest[:2]
    lanes, (held, picked) = rest[2:2 + LANES], rest[2 + LANES:]
    take_lanes(z, arrived, held)
    coarse_in_kernel(z, small_a[...] + small_b[...], coarse, pick, picked)
    for face in range(z.total):
        value = image_of_face(z, tab, face, image, held, picked, spread)
        residual[face] = value
        weighted[face] = jnp.dot(value.astype(BF), blocks[face], preferred_element_type=F32)
    fill_lanes(z, tab, weighted, lanes)


def step_kernel(first, last, z, tab, image, small_a, small_b, coarse, pick, spread, blocks, vec, old_residual, *rest):
    if not first:
        old_solution, old_direction, old_image, old_scalars = rest[:4]
        rest = rest[4:]
    arrived, rest = rest[:LANES], rest[LANES:]
    solution_out, residual = rest[:2]
    rest = rest[2:]
    if not last:
        direction, new_image, scalars, weighted = rest[:4]
        lanes, rest = rest[4:4 + LANES], rest[4 + LANES:]
    held, picked = rest
    take_lanes(z, arrived, held)
    small = small_a[...] + small_b[...]
    energy = coarse_in_kernel(z, small, coarse, pick, picked)
    gamma = small[:, z.coarse:z.coarse + 1]
    kappa = small[:, z.coarse + 1:z.coarse + 2]
    eta = small[:, z.coarse + 2:z.coarse + 3]
    curvature = 2.0 * (kappa + energy)
    beta = None
    if not first:
        beta = gamma / old_scalars[:, 0:1]
        curvature = curvature + beta * (2.0 * eta + beta * old_scalars[:, 1:2])
    alpha = gamma / curvature
    if not last:
        column = lax.broadcasted_iota(jnp.int32, (z.loads, WIDE), 1)
        scalars[...] = jnp.where(column == 0, gamma, curvature)
    wide = (z.loads, z.dof)
    alpha_wide = jnp.broadcast_to(alpha, wide)
    beta_wide = None if first else jnp.broadcast_to(beta, wide)
    for face in range(z.total):
        ahead = image_of_face(z, tab, face, image, held, picked, spread)
        along = vec[face]
        if not first:
            ahead = ahead + beta_wide * old_image[face]
            along = along + beta_wide * old_direction[face]
        moved = alpha_wide * along
        solution_out[face] = moved if first else old_solution[face] + moved
        value = old_residual[face] - alpha_wide * ahead
        residual[face] = value
        if not last:
            direction[face] = along
            new_image[face] = ahead
            weighted[face] = jnp.dot(value.astype(BF), blocks[face], preferred_element_type=F32)
    if not last:
        fill_lanes(z, tab, weighted, lanes)


def exchange(lanes, devices):
    return [lax.ppermute(lane, "sub", pairs) for lane, pairs in zip(lanes, lane_pairs(devices))]


def summed_shares(small, devices):
    def other(value, pairs):
        return lax.ppermute(value, "sub", pairs)

    core = lax.axis_index("sub") % 2
    chip = small + other(small, flipped(1, devices))
    plane = chip + other(chip, flipped(2, devices))
    if devices == 4:
        return plane, jnp.zeros_like(plane)
    near = other(plane, [(i, i ^ (8 if i % 2 else 4)) for i in range(devices)])
    far = other(plane, flipped(12, devices))
    half = near + jnp.where(core == 0, plane, far)
    rest = other(half, flipped(1, devices))
    mask = 16
    while mask < devices:
        whole = half + rest
        half, rest = whole, other(whole, flipped(mask, devices))
        mask *= 2
    return half, rest


def on_device(load, stiff_inv, face_blocks, coupling, coarse_inv, corners, partner):
    devices = lax.axis_size("sub")
    z = Sizes(load, coupling, coarse_inv)
    coarse = lax.all_gather(coarse_inv, "sub", axis=0, tiled=True)
    tab = routing(partner, z.slots_per_lane)

    numbers = jnp.pad(corners.astype(F32), ((0, 0), (0, PAD - z.primal)), constant_values=-1.0)
    row = jnp.pad(numbers.reshape(1, -1), ((0, 0), (0, WIDE - z.subs * PAD)), constant_values=-1.0)
    corner_row = jnp.broadcast_to(row, (8, WIDE))
    twice = jnp.stack([numbers, numbers], axis=1).reshape(-1)
    spot = (twice[:, None] == jnp.arange(z.coarse, dtype=F32)[None, :]).astype(BF)

    field = shape(z.total, z.loads, z.dof)
    lane_field = [shape(z.slots_per_lane, z.loads, z.dof)] * LANES
    small_shape = shape(z.loads, z.small_width)
    held = pltpu.VMEM((z.slots, z.loads, z.dof), F32)
    picked = pltpu.VMEM((z.blocks, z.loads, WIDE), BF)
    apply_scratch = [
        pltpu.VMEM((z.subs, z.unknowns, z.unknowns), BF),
        pltpu.VMEM((z.subs, 2 * z.loads, z.unknowns), BF),
        pltpu.SemaphoreType.DMA((z.subs * 8,)),
    ]
    apply_cost = dict(flops=2 * z.total * z.dof * z.unknowns * z.loads, moved=stiff_inv.size * 2)

    packed = call(
        pack_kernel, z,
        [shape(z.carry_rows, z.dof)] * LANES + [shape(z.subs, 4 * PAD, z.unknowns, dtype=BF)],
        (tab, coupling, corner_row), [SMEM, VMEM, VMEM], [], 16, "pack_coupling",
    )
    weights = packed[LANES]
    carried = exchange(packed[:LANES], devices)

    load_faces = load.reshape(z.total, z.loads, z.dof)
    image, small, *lanes = call(
        load_kernel, z, [field, small_shape] + lane_field,
        (tab, load_faces, weights, spot, stiff_inv), [SMEM, VMEM, VMEM, VMEM, HBM],
        apply_scratch, 32, "apply_load", **apply_cost,
    )
    spread, pick = call(
        unpack_kernel, z,
        [shape(z.total, 8 * PAD, z.dof, dtype=BF), shape(z.coarse, z.pick_width, dtype=BF)],
        (tab, coupling, corner_row, *carried), [SMEM] + [VMEM] * (2 + LANES),
        [pltpu.VMEM((z.slots, z.primal, z.dof), F32), pltpu.VMEM((8, z.pick_width), F32)],
        16, "unpack_coupling",
    )
    blocks = face_blocks.reshape(z.total, z.dof, z.dof)

    arrived = exchange(lanes, devices)
    share_a, share_b = summed_shares(small, devices)
    fixed = (coarse, pick, spread, blocks)
    residual, weighted, *lanes = call(
        start_kernel, z, [field, field] + lane_field,
        (tab, image, share_a, share_b, *fixed, *arrived), [SMEM] + [VMEM] * (7 + LANES),
        [held, picked], 24, "first_residual",
    )
    state = None
    for iteration in range(ITERS):
        first, last = iteration == 0, iteration + 1 == ITERS
        arrived = exchange(lanes, devices)
        old_image = residual if first else state[2]
        vec, image, small, *lanes = call(
            precond_kernel, z, [field, field, small_shape] + lane_field,
            (tab, weighted, residual, old_image, weights, spot, stiff_inv, *arrived),
            [SMEM] + [VMEM] * 5 + [HBM] + [VMEM] * LANES,
            apply_scratch + [held], 32, "precond_apply", **apply_cost,
        )
        arrived = exchange(lanes, devices)
        share_a, share_b = summed_shares(small, devices)
        ins = [tab, image, share_a, share_b, *fixed, vec, residual] + ([] if first else list(state)) + list(arrived)
        outs = [field, field] + ([] if last else [field, field, shape(z.loads, WIDE), field] + lane_field)
        result = call(
            functools.partial(step_kernel, first, last), z, outs, ins, [SMEM] + [VMEM] * (len(ins) - 1),
            [held, picked], 24, "cg_step",
        )
        multipliers, residual = result[:2]
        if not last:
            direction, old, scalars, weighted = result[2:6]
            lanes = result[6:]
            state = (multipliers, direction, old, scalars)
    return multipliers.reshape(load.shape), residual.reshape(load.shape)


def solution(mesh):
    return jax.shard_map(
        on_device,
        mesh=mesh,
        in_specs=(
            P(("parts", "sub"), None, None, None),
            P(("parts", "sub"), None, None),
            P(("parts", "sub"), None, None, None),
            P(("parts", "sub"), None, None),
            P(("parts", "sub"), None),
            P(("parts", "sub"), None),
            P(("parts", "sub"), None),
        ),
        out_specs=(P(("parts", "sub"), None, None, None), P(("parts", "sub"), None, None, None)),
        check_vma=False,
    )
```

```python
import functools
import jax
import jax.numpy as jnp
from jax import lax
from jax.experimental import pallas as pl
from jax.experimental.pallas import tpu as pltpu
from jax.sharding import PartitionSpec as P

ITERS = 3
LANES = 6
PAD = 32
WIDE = 128
BF = jnp.bfloat16
F32 = jnp.float32
VMEM = pl.BlockSpec(memory_space=pltpu.VMEM)
SMEM = pl.BlockSpec(memory_space=pltpu.SMEM)
HBM = pl.BlockSpec(memory_space=pltpu.HBM)
PARTS = 8
FIRST_LIMIT = 31
NT = (((1,), (1,)), ((), ()))


def matching(pairs, rest):
    both = list(pairs) + list(rest)
    return sorted(both + [(second, first) for first, second in both])


def flipped(mask, devices):
    return [(i, i ^ mask) for i in range(devices)]


def lane_pairs(devices):
    odd = range(2, devices - 2, 4)
    ends = [(0, 1), (devices - 2, devices - 1)]
    return (
        flipped(2, devices),
        flipped(3, devices),
        matching([(i + core, i + 2 + core) for i in odd for core in (0, 1)], ends),
        matching([(i + core, i + 3 - core) for i in odd for core in (0, 1)], ends),
        matching([(i, i + 3) for i in range(1, devices - 3, 2)], [(0, devices - 3), (2, devices - 1)]),
        flipped(1, devices),
    )


def split_hi_lo(value):
    high = value.astype(BF)
    return high, (value - high.astype(F32)).astype(BF)


def routing(partner, capacity):
    face_count = partner.size
    subs = partner.shape[0]
    own = lax.axis_index("sub")
    ids = partner.reshape(face_count)
    peer = ids // face_count
    chip_gap = jnp.abs(peer // 2 - own // 2)
    lowest = jnp.minimum(peer // 2, own // 2)
    crossed = (peer + own) % 2
    lane = jnp.where(chip_gap == 0, 5, jnp.where(chip_gap == 1, 2 * (lowest % 2) + crossed, 4))
    order = jnp.arange(face_count, dtype=jnp.int32)
    same = lane[:, None] == lane[None, :]
    send_pos = jnp.sum(same & (order[None, :] < order[:, None]), axis=1, dtype=jnp.int32)
    recv_pos = jnp.sum(same & (ids[None, :] < ids[:, None]), axis=1, dtype=jnp.int32)
    slots = jnp.arange(LANES * capacity, dtype=jnp.int32)
    hit = slots[:, None] == (lane * capacity + send_pos)[None, :]
    source = jnp.sum(jnp.where(hit, order[None, :], 0), axis=1, dtype=jnp.int32)
    arrival = lane * capacity + recv_pos
    block = (1 + lane) * subs + (ids // partner.shape[1]) % subs
    return jnp.concatenate([source, arrival, block]).astype(jnp.int32)


class Sizes:
    def __init__(self, load, coupling, coarse_inv, devices):
        self.planes = devices // 4
        self.subs, self.faces, self.loads, self.dof = load.shape
        self.total = self.subs * self.faces
        self.unknowns = self.faces * self.dof
        self.slots_per_lane = 3 * self.total // 8
        self.slots = LANES * self.slots_per_lane
        self.primal = coupling.shape[1]
        self.coarse = coarse_inv.shape[1]
        self.own_rows = coarse_inv.shape[0]
        self.blocks = (1 + LANES) * self.subs
        self.pick_width = -(-self.blocks * PAD // WIDE) * WIDE
        self.carry_rows = self.slots_per_lane * (self.loads + self.primal) + 8


def call(kernel, sizes, outs, ins, specs, scratch, limit, name, flops=0, moved=0):
    return pl.pallas_call(
        functools.partial(kernel, sizes),
        out_shape=outs,
        in_specs=specs,
        out_specs=[VMEM] * len(outs),
        scratch_shapes=scratch,
        compiler_params=pltpu.CompilerParams(vmem_limit_bytes=limit * 2**20),
        cost_estimate=pl.CostEstimate(flops=flops, bytes_accessed=moved, transcendentals=0),
        name=name,
    )(*ins)


def shape(*dims, dtype=F32):
    return jax.ShapeDtypeStruct(dims, dtype)


def unpack_kernel(z, tab, coupling, corner_row, *rest):
    arrived, rest = rest[:LANES], rest[LANES:]
    spread, pick, held, names = rest
    per = z.slots_per_lane
    width = z.subs * PAD
    names[...] = jnp.full(names.shape, -1.0, F32)
    names[:, 0:width] = corner_row[:, 0:width]
    for lane in range(LANES):
        names[:, (1 + lane) * width:(2 + lane) * width] = arrived[lane][per * (z.loads + z.primal):per * (z.loads + z.primal) + 8, 0:width]
        for pos in range(per):
            row = per * z.loads + pos * z.primal
            held[lane * per + pos] = arrived[lane][row:row + z.primal, :]
    rows = lax.broadcasted_iota(jnp.int32, pick.shape, 0).astype(F32)
    pick[...] = jnp.where(rows == names[0:1, :], 1.0, 0.0).astype(BF)
    gap = jnp.zeros((PAD - z.primal, z.dof), F32)
    blank = jnp.zeros((PAD, z.dof), BF)
    for face in range(z.total):
        sub, side = face // z.faces, face % z.faces
        own = coupling[sub, :, side * z.dof:(side + 1) * z.dof]
        other = -held[tab[z.slots + face]]
        for place, value in enumerate((own, other)):
            high, low = split_hi_lo(jnp.concatenate([value, gap], axis=0))
            spread[face, place * 4 * PAD:(place + 1) * 4 * PAD, :] = jnp.concatenate([high, low, high, blank], axis=0)


def assemble_kernel(masks, z, own, *rest):
    stacks, (upper, lower) = rest[:len(masks)], rest[len(masks):]
    count = z.own_rows
    for mask, stack in zip(masks, stacks):
        for place, flip in enumerate((mask, mask ^ 2)):
            start = pl.multiple_of((own[0] ^ flip) * count, count)
            high, low = split_hi_lo(stack[place * count:(place + 1) * count, :])
            upper[pl.ds(start, count), :] = high
            lower[pl.ds(start, count), :] = low


def apply_in_kernel(z, vec, scalars, weights, stiff, copies, packed, image, shares):
    for face in range(z.total):
        sub, side = face // z.faces, face % z.faces
        high, low = split_hi_lo(vec[face])
        packed[sub, 0:z.loads, side * z.dof:(side + 1) * z.dof] = high
        packed[sub, z.loads:, side * z.dof:(side + 1) * z.dof] = low
    n = z.loads
    rows = jnp.zeros((2 * n, WIDE), F32)
    for sub in range(z.subs):
        rows = rows + lax.dot_general(packed[sub], weights[sub], NT, preferred_element_type=F32)
    rows = rows[0:n] + rows[n:]
    rows = rows + pltpu.roll(rows, WIDE - PAD, 1)
    step = z.unknowns // PARTS
    kappa = jnp.zeros((n, z.dof), F32)
    for sub in range(z.subs):
        total = jnp.zeros((2 * n, z.unknowns), F32)
        for part in range(PARTS):
            if copies:
                copies[sub * PARTS + part].wait()
            total = total + jnp.dot(
                packed[sub, :, part * step:(part + 1) * step],
                stiff[sub, part * step:(part + 1) * step, :],
                preferred_element_type=F32,
            )
        total = total[0:n] + total[n:]
        for side in range(z.faces):
            piece = total[:, side * z.dof:(side + 1) * z.dof]
            image[sub * z.faces + side] = piece
            kappa = kappa + piece * vec[sub * z.faces + side]
    column = lax.broadcasted_iota(jnp.int32, (n, WIDE), 1)
    share = jnp.where(column % (2 * PAD) < PAD, rows, 0.0)
    for place, value in enumerate([kappa] + scalars):
        share = jnp.where(column == PAD + place, jnp.sum(value, axis=1, keepdims=True), share)
    shares[0:n, :] = share


def fill_lanes(z, tab, field, lanes):
    for lane in range(LANES):
        for pos in range(z.slots_per_lane):
            lanes[lane][pos] = field[tab[lane * z.slots_per_lane + pos]]


def take_lanes(z, arrived, held):
    per = z.slots_per_lane
    for lane in range(LANES):
        held[lane * per:(lane + 1) * per] = arrived[lane][0:per]


def load_kernel(z, tab, load, coupling, corner_row, corner_groups, stiff, image, shares, *rest):
    lanes, (near, weights, packed, sems) = rest[:LANES], rest[LANES:]
    step = z.unknowns // PARTS
    copies = [
        pltpu.make_async_copy(
            stiff.at[sub, pl.ds(part * step, step), :],
            near.at[sub, pl.ds(part * step, step), :],
            sems.at[sub * PARTS + part],
        )
        for sub in range(z.subs)
        for part in range(PARTS)
    ]
    for copy in copies:
        copy.start()
    per = z.slots_per_lane
    base = per * z.loads
    for lane in range(LANES):
        for pos in range(per):
            face = tab[lane * per + pos]
            sub = face // z.faces
            start = pl.multiple_of((face - sub * z.faces) * z.dof, z.dof)
            row = base + pos * z.primal
            lanes[lane][row:row + z.primal, :] = coupling[sub, :, pl.ds(start, z.dof)]
        lanes[lane][base + per * z.primal:z.carry_rows, :] = corner_row[...]
    weights[...] = jnp.zeros_like(weights)
    gap = jnp.zeros((PAD - z.primal, z.unknowns), F32)
    for sub in range(z.subs):
        high, low = split_hi_lo(jnp.concatenate([coupling[sub], gap], axis=0))
        weights[sub, sub * 2 * PAD:sub * 2 * PAD + PAD, :] = high
        weights[sub, sub * 2 * PAD + PAD:sub * 2 * PAD + 2 * PAD, :] = low
    apply_in_kernel(z, load, [], weights, near, copies, packed, image, shares)
    shares[z.loads:, :] = corner_groups[...]
    for lane in range(LANES):
        for pos in range(per):
            lanes[lane][pos * z.loads:(pos + 1) * z.loads, :] = image[tab[lane * per + pos]]


def precond_kernel(z, tab, weighted, residual, old_image, weights, stiff, *rest):
    arrived, rest = rest[:LANES], rest[LANES:]
    vec, image, shares = rest[:3]
    lanes, (packed, held) = rest[3:3 + LANES], rest[3 + LANES:]
    take_lanes(z, arrived, held)
    gamma = jnp.zeros((z.loads, z.dof), F32)
    eta = jnp.zeros((z.loads, z.dof), F32)
    for face in range(z.total):
        value = 0.25 * (weighted[face] - held[tab[z.slots + face]])
        vec[face] = value
        gamma = gamma + residual[face] * value
        eta = eta + old_image[face] * value
    apply_in_kernel(z, vec, [gamma, eta], weights, stiff, None, packed, image, shares)
    fill_lanes(z, tab, image, lanes)


def coarse_in_kernel(z, shares, spot, inv_high, inv_low, pick, picked):
    n = z.loads
    rows = [stack[place, 0:n] for stack in shares for place in range(4)]
    high, low = split_hi_lo(jnp.concatenate(rows, axis=1))
    together = rows
    while len(together) > 1:
        together = [first + second for first, second in zip(together[0::2], together[1::2])]
    primal = jnp.dot(jnp.concatenate([high, low], axis=0), spot[...], preferred_element_type=F32)
    primal = primal[0:n] + primal[n:]
    high, low = split_hi_lo(primal)
    both = jnp.dot(jnp.concatenate([high, low], axis=0), inv_high[...], preferred_element_type=F32)
    lifted = (both[0:n] + both[n:]) + jnp.dot(high, inv_low[...], preferred_element_type=F32)
    energy = jnp.sum(primal * lifted, axis=1, keepdims=True)
    high, low = split_hi_lo(lifted)
    values = jnp.dot(jnp.concatenate([high, low], axis=0), pick[...], preferred_element_type=F32)
    column = lax.broadcasted_iota(jnp.int32, (n, WIDE), 1)
    for block in range(z.blocks):
        group, place = divmod(block * PAD, WIDE)
        upper = values[0:n, group * WIDE:(group + 1) * WIDE]
        lower = values[n:, group * WIDE:(group + 1) * WIDE]
        first = pltpu.roll(upper, (WIDE - place) % WIDE, 1)
        second = pltpu.roll(upper, (WIDE + PAD - place) % WIDE, 1)
        third = pltpu.roll(lower, (WIDE + 2 * PAD - place) % WIDE, 1)
        mixed = jnp.where(column < PAD, first, jnp.where(column < 2 * PAD, second, third))
        picked[block] = jnp.where(column < 3 * PAD, mixed, 0.0).astype(BF)
    return energy, together[0]


def image_of_face(z, tab, face, image, held, picked, spread):
    sides = jnp.concatenate([picked[face // z.faces], picked[tab[z.slots + z.total + face]]], axis=1)
    lift = jnp.dot(sides, spread[face], preferred_element_type=F32)
    return (image[face] - held[tab[z.slots + face]]) + lift


def start_kernel(z, tab, image, spot, upper, lower, pick, spread, blocks, *rest):
    shares, rest = rest[:z.planes], rest[z.planes:]
    arrived, rest = rest[:LANES], rest[LANES:]
    residual, weighted = rest[:2]
    lanes, (held, picked) = rest[2:2 + LANES], rest[2 + LANES:]
    for lane in range(LANES):
        for pos in range(z.slots_per_lane):
            held[lane * z.slots_per_lane + pos] = arrived[lane][pos * z.loads:(pos + 1) * z.loads, :]
    coarse_in_kernel(z, shares, spot, upper, lower, pick, picked)
    for face in range(z.total):
        value = image_of_face(z, tab, face, image, held, picked, spread)
        residual[face] = value
        weighted[face] = jnp.dot(value.astype(BF), blocks[face], preferred_element_type=F32)
    fill_lanes(z, tab, weighted, lanes)


def step_kernel(first, last, z, tab, image, spot, upper, lower, pick, spread, blocks, vec, old_residual, *rest):
    shares, rest = rest[:z.planes], rest[z.planes:]
    if not first:
        old_solution, old_direction, old_image, old_scalars = rest[:4]
        rest = rest[4:]
    arrived, rest = rest[:LANES], rest[LANES:]
    solution_out, residual = rest[:2]
    rest = rest[2:]
    if not last:
        direction, new_image, scalars, weighted = rest[:4]
        lanes, rest = rest[4:4 + LANES], rest[4 + LANES:]
    held, picked = rest
    take_lanes(z, arrived, held)
    energy, together = coarse_in_kernel(z, shares, spot, upper, lower, pick, picked)
    kappa, gamma, eta = [together[:, PAD + place:PAD + place + 1] for place in range(3)]
    curvature = 2.0 * (kappa + energy)
    beta = None
    if not first:
        beta = gamma / old_scalars[:, 0:1]
        curvature = curvature + beta * (2.0 * eta + beta * old_scalars[:, 1:2])
    alpha = gamma / curvature
    if not last:
        column = lax.broadcasted_iota(jnp.int32, (z.loads, WIDE), 1)
        scalars[...] = jnp.where(column == 0, gamma, curvature)
    wide = (z.loads, z.dof)
    alpha_wide = jnp.broadcast_to(alpha, wide)
    beta_wide = None if first else jnp.broadcast_to(beta, wide)
    for face in range(z.total):
        ahead = image_of_face(z, tab, face, image, held, picked, spread)
        along = vec[face]
        if not first:
            ahead = ahead + beta_wide * old_image[face]
            along = along + beta_wide * old_direction[face]
        moved = alpha_wide * along
        solution_out[face] = moved if first else old_solution[face] + moved
        value = old_residual[face] - alpha_wide * ahead
        residual[face] = value
        if not last:
            direction[face] = along
            new_image[face] = ahead
            weighted[face] = jnp.dot(value.astype(BF), blocks[face], preferred_element_type=F32)
    if not last:
        fill_lanes(z, tab, weighted, lanes)


def exchange(lanes, devices):
    return [lax.ppermute(lane, "sub", pairs) for lane, pairs in zip(lanes, lane_pairs(devices))]


def gathered(rows, devices):
    pair = jnp.concatenate([rows, lax.ppermute(rows, "sub", flipped(2, devices))])
    stacks = [(0, pair)] + [(mask, lax.ppermute(pair, "sub", flipped(mask, devices))) for mask in range(4, devices, 4)]
    return stacks + [(mask ^ 1, lax.ppermute(stack, "sub", flipped(1, devices))) for mask, stack in stacks]


def gathered_shares(share, devices):
    def other(value, mask):
        return lax.ppermute(value, "sub", flipped(mask, devices))

    plane = jnp.stack([share, other(share, 1), other(share, 2), other(share, 3)])
    return [plane] + [other(plane, mask) for mask in range(4, devices, 4)]


def on_device(load, stiff_inv, face_blocks, coupling, coarse_inv, corners, partner):
    devices = lax.axis_size("sub")
    z = Sizes(load, coupling, coarse_inv, devices)
    stacks = gathered(coarse_inv, devices)
    masks = tuple(mask for mask, _ in stacks)
    stacks = [stack for _, stack in stacks]
    tab = routing(partner, z.slots_per_lane)

    numbers = jnp.pad(corners.astype(F32), ((0, 0), (0, PAD - z.primal)), constant_values=-1.0)
    row = jnp.pad(numbers.reshape(1, -1), ((0, 0), (0, WIDE - z.subs * PAD)), constant_values=-1.0)
    corner_row = jnp.broadcast_to(row, (8, WIDE))
    apart = jnp.pad(numbers, ((0, 0), (0, WIDE // z.subs - PAD)), constant_values=-1.0)
    corner_groups = jnp.broadcast_to(apart.reshape(1, WIDE), (8, WIDE))

    field = shape(z.total, z.loads, z.dof)
    lane_field = [shape(z.slots_per_lane, z.loads, z.dof)] * LANES
    held = pltpu.VMEM((z.slots, z.loads, z.dof), F32)
    picked = pltpu.VMEM((z.blocks, z.loads, WIDE), BF)
    apply_scratch = [pltpu.VMEM((z.subs, 2 * z.loads, z.unknowns), BF)]
    apply_cost = dict(flops=2 * z.total * z.dof * z.unknowns * z.loads, moved=stiff_inv.size * 2)

    load_faces = load.reshape(z.total, z.loads, z.dof)
    image, shares, *lanes = call(
        load_kernel, z,
        [field, shape(z.loads + 8, WIDE)]
        + [shape(z.carry_rows, z.dof)] * LANES
        + [shape(z.subs, z.unknowns, z.unknowns, dtype=BF), shape(z.subs, 4 * PAD, z.unknowns, dtype=BF)],
        (tab, load_faces, coupling, corner_row, corner_groups, stiff_inv), [SMEM] + [VMEM] * 4 + [HBM],
        apply_scratch + [pltpu.SemaphoreType.DMA((z.subs * PARTS,))], FIRST_LIMIT, "apply_load", **apply_cost,
    )
    near, weights = lanes[LANES:]
    shares = gathered_shares(shares, devices)
    arrived = exchange(lanes[:LANES], devices)
    names = jnp.concatenate([stack[:, z.loads, :] for stack in shares]).reshape(-1)
    spot = (names[:, None] == jnp.arange(z.coarse, dtype=F32)[None, :]).astype(BF)
    spread, pick = call(
        unpack_kernel, z,
        [shape(z.total, 8 * PAD, z.dof, dtype=BF), shape(z.coarse, z.pick_width, dtype=BF)],
        (tab, coupling, corner_row, *arrived), [SMEM] + [VMEM] * (2 + LANES),
        [pltpu.VMEM((z.slots, z.primal, z.dof), F32), pltpu.VMEM((8, z.pick_width), F32)],
        8, "unpack_coupling",
    )
    blocks = face_blocks.reshape(z.total, z.dof, z.dof)
    inv_shape = shape(z.coarse, z.coarse, dtype=BF)
    upper, lower = call(
        functools.partial(assemble_kernel, masks), z, [inv_shape, inv_shape],
        (lax.axis_index("sub").reshape(1).astype(jnp.int32), *stacks),
        [SMEM] + [VMEM] * len(masks), [], 8, "assemble_coarse",
    )
    fixed = (spot, upper, lower, pick, spread, blocks)
    residual, weighted, *lanes = call(
        start_kernel, z, [field, field] + lane_field,
        (tab, image, *fixed, *shares, *arrived), [SMEM] + [VMEM] * (7 + z.planes + LANES),
        [held, picked], 8, "first_residual",
    )
    state = None
    for iteration in range(ITERS):
        first, last = iteration == 0, iteration + 1 == ITERS
        arrived = exchange(lanes, devices)
        old_image = residual if first else state[2]
        vec, image, shares, *lanes = call(
            precond_kernel, z, [field, field, shape(z.loads, WIDE)] + lane_field,
            (tab, weighted, residual, old_image, weights, near, *arrived),
            [SMEM] + [VMEM] * (5 + LANES),
            apply_scratch + [held], 8, "precond_apply", **apply_cost,
        )
        shares = gathered_shares(shares, devices)
        arrived = exchange(lanes, devices)
        ins = [tab, image, *fixed, vec, residual, *shares] + ([] if first else list(state)) + list(arrived)
        outs = [field, field] + ([] if last else [field, field, shape(z.loads, WIDE), field] + lane_field)
        result = call(
            functools.partial(step_kernel, first, last), z, outs, ins, [SMEM] + [VMEM] * (len(ins) - 1),
            [held, picked], 8, "cg_step",
        )
        multipliers, residual = result[:2]
        if not last:
            direction, old, scalars, weighted = result[2:6]
            lanes = result[6:]
            state = (multipliers, direction, old, scalars)
    return multipliers.reshape(load.shape), residual.reshape(load.shape)


def solution(mesh):
    return jax.shard_map(
        on_device,
        mesh=mesh,
        in_specs=(
            P(("parts", "sub"), None, None, None),
            P(("parts", "sub"), None, None),
            P(("parts", "sub"), None, None, None),
            P(("parts", "sub"), None, None),
            P(("parts", "sub"), None),
            P(("parts", "sub"), None),
            P(("parts", "sub"), None),
        ),
        out_specs=(P(("parts", "sub"), None, None, None), P(("parts", "sub"), None, None, None)),
        check_vma=False,
    )
```

```python
import functools
import jax
import jax.numpy as jnp
from jax import lax
from jax.experimental import pallas as pl
from jax.experimental.pallas import tpu as pltpu
from jax.sharding import PartitionSpec as P

ITERS = 3
LANES = 6
EARLY = (0, 1, 5)
PAD = 32
WIDE = 128
BF = jnp.bfloat16
F32 = jnp.float32
VMEM = pl.BlockSpec(memory_space=pltpu.VMEM)
SMEM = pl.BlockSpec(memory_space=pltpu.SMEM)
HBM = pl.BlockSpec(memory_space=pltpu.HBM)
PARTS = 8
FIRST_LIMIT = 31
NT = (((1,), (1,)), ((), ()))


def matching(pairs, rest):
    both = list(pairs) + list(rest)
    return sorted(both + [(second, first) for first, second in both])


def flipped(mask, devices):
    return [(i, i ^ mask) for i in range(devices)]


def lane_pairs(devices):
    odd = range(2, devices - 2, 4)
    ends = [(0, 1), (devices - 2, devices - 1)]
    return (
        flipped(2, devices),
        flipped(3, devices),
        matching([(i + core, i + 2 + core) for i in odd for core in (0, 1)], ends),
        matching([(i + core, i + 3 - core) for i in odd for core in (0, 1)], ends),
        matching([(i, i + 3) for i in range(1, devices - 3, 2)], [(0, devices - 3), (2, devices - 1)]),
        flipped(1, devices),
    )


def split_hi_lo(value):
    high = value.astype(BF)
    return high, (value - high.astype(F32)).astype(BF)


def routing(partner, capacity):
    face_count = partner.size
    subs = partner.shape[0]
    own = lax.axis_index("sub")
    ids = partner.reshape(face_count)
    peer = ids // face_count
    chip_gap = jnp.abs(peer // 2 - own // 2)
    lowest = jnp.minimum(peer // 2, own // 2)
    crossed = (peer + own) % 2
    lane = jnp.where(chip_gap == 0, 5, jnp.where(chip_gap == 1, 2 * (lowest % 2) + crossed, 4))
    order = jnp.arange(face_count, dtype=jnp.int32)
    same = lane[:, None] == lane[None, :]
    send_pos = jnp.sum(same & (order[None, :] < order[:, None]), axis=1, dtype=jnp.int32)
    recv_pos = jnp.sum(same & (ids[None, :] < ids[:, None]), axis=1, dtype=jnp.int32)
    slots = jnp.arange(LANES * capacity, dtype=jnp.int32)
    hit = slots[:, None] == (lane * capacity + send_pos)[None, :]
    source = jnp.sum(jnp.where(hit, order[None, :], 0), axis=1, dtype=jnp.int32)
    arrival = lane * capacity + recv_pos
    block = (1 + lane) * subs + (ids // partner.shape[1]) % subs
    return jnp.concatenate([source, arrival, block]).astype(jnp.int32)


class Sizes:
    def __init__(self, load, coupling, coarse_inv, devices):
        self.subs, self.faces, self.loads, self.dof = load.shape
        self.total = self.subs * self.faces
        self.unknowns = self.faces * self.dof
        self.slots_per_lane = 3 * self.total // 8
        self.slots = LANES * self.slots_per_lane
        self.primal = coupling.shape[1]
        self.coarse = coarse_inv.shape[1]
        self.own_rows = coarse_inv.shape[0]
        self.groups = self.coarse // WIDE
        self.blocks = (1 + LANES) * self.subs
        self.pick_width = -(-self.blocks * PAD // WIDE) * WIDE
        self.carry_rows = self.slots_per_lane * (self.loads + self.primal) + 8


def call(kernel, sizes, outs, ins, specs, scratch, limit, name, flops=0, moved=0):
    return pl.pallas_call(
        functools.partial(kernel, sizes),
        out_shape=outs,
        in_specs=specs,
        out_specs=[VMEM] * len(outs),
        scratch_shapes=scratch,
        compiler_params=pltpu.CompilerParams(vmem_limit_bytes=limit * 2**20),
        cost_estimate=pl.CostEstimate(flops=flops, bytes_accessed=moved, transcendentals=0),
        name=name,
    )(*ins)


def shape(*dims, dtype=F32):
    return jax.ShapeDtypeStruct(dims, dtype)


def unpack_kernel(z, tab, coupling, corner_row, *rest):
    arrived, rest = rest[:LANES], rest[LANES:]
    spread, pick, held, names = rest
    per = z.slots_per_lane
    width = z.subs * PAD
    names[...] = jnp.full(names.shape, -1.0, F32)
    names[:, 0:width] = corner_row[:, 0:width]
    for lane in range(LANES):
        names[:, (1 + lane) * width:(2 + lane) * width] = arrived[lane][per * (z.loads + z.primal):per * (z.loads + z.primal) + 8, 0:width]
        for pos in range(per):
            row = per * z.loads + pos * z.primal
            held[lane * per + pos] = arrived[lane][row:row + z.primal, :]
    rows = lax.broadcasted_iota(jnp.int32, pick.shape, 0).astype(F32)
    pick[...] = jnp.where(rows == names[0:1, :], 1.0, 0.0).astype(BF)
    gap = jnp.zeros((PAD - z.primal, z.dof), F32)
    blank = jnp.zeros((PAD, z.dof), BF)
    for face in range(z.total):
        sub, side = face // z.faces, face % z.faces
        own = coupling[sub, :, side * z.dof:(side + 1) * z.dof]
        other = -held[tab[z.slots + face]]
        for place, value in enumerate((own, other)):
            high, low = split_hi_lo(jnp.concatenate([value, gap], axis=0))
            spread[face, place * 4 * PAD:(place + 1) * 4 * PAD, :] = jnp.concatenate([high, low, high, blank], axis=0)


def assemble_kernel(masks, z, own, *rest):
    stacks, (upper, lower) = rest[:len(masks)], rest[len(masks):]
    count = z.own_rows
    for mask, stack in zip(masks, stacks):
        for place, flip in enumerate((mask, mask ^ 2)):
            start = pl.multiple_of((own[0] ^ flip) * count, count)
            high, low = split_hi_lo(stack[place * count:(place + 1) * count, :])
            upper[pl.ds(start, count), :] = high
            lower[pl.ds(start, count), :] = low


def apply_in_kernel(z, vec, scalars, weights, spot, stiff, copies, packed, image, small):
    for face in range(z.total):
        sub, side = face // z.faces, face % z.faces
        high, low = split_hi_lo(vec[face])
        packed[sub, 0:z.loads, side * z.dof:(side + 1) * z.dof] = high
        packed[sub, z.loads:, side * z.dof:(side + 1) * z.dof] = low
    n = z.loads
    rows = jnp.zeros((2 * n, WIDE), F32)
    for sub in range(z.subs):
        rows = rows + lax.dot_general(packed[sub], weights[sub], NT, preferred_element_type=F32)
    rows = rows[0:n] + rows[n:]
    rows = rows + pltpu.roll(rows, WIDE - PAD, 1)
    column = lax.broadcasted_iota(jnp.int32, (n, WIDE), 1)
    rows = jnp.where(column % (2 * PAD) < PAD, rows, 0.0)
    summed = jnp.dot(jnp.concatenate(split_hi_lo(rows), axis=0), spot[...], preferred_element_type=F32)
    summed = summed[0:n] + summed[n:]
    for group in range(z.groups):
        small[group] = summed[:, group * WIDE:(group + 1) * WIDE]
    step = z.unknowns // PARTS
    kappa = jnp.zeros((n, z.dof), F32)
    for sub in range(z.subs):
        total = jnp.zeros((2 * n, z.unknowns), F32)
        for part in range(PARTS):
            if copies:
                copies[sub * PARTS + part].wait()
            total = total + jnp.dot(
                packed[sub, :, part * step:(part + 1) * step],
                stiff[sub, part * step:(part + 1) * step, :],
                preferred_element_type=F32,
            )
        total = total[0:n] + total[n:]
        for side in range(z.faces):
            piece = total[:, side * z.dof:(side + 1) * z.dof]
            image[sub * z.faces + side] = piece
            kappa = kappa + piece * vec[sub * z.faces + side]
    tail = jnp.zeros((n, WIDE), F32)
    for place, value in enumerate([kappa] + scalars):
        tail = jnp.where(column == place, jnp.sum(value, axis=1, keepdims=True), tail)
    small[z.groups] = tail


def fill_lanes(z, tab, field, lanes):
    for lane in range(LANES):
        for pos in range(z.slots_per_lane):
            lanes[lane][pos] = field[tab[lane * z.slots_per_lane + pos]]


def take_lanes(z, arrived, held):
    per = z.slots_per_lane
    for lane in range(LANES):
        held[lane * per:(lane + 1) * per] = arrived[lane][0:per]


def load_kernel(z, tab, load, coupling, corner_row, spot, stiff, image, small, *rest):
    lanes, (near, weights, packed, sems) = rest[:LANES], rest[LANES:]
    step = z.unknowns // PARTS
    copies = [
        pltpu.make_async_copy(
            stiff.at[sub, pl.ds(part * step, step), :],
            near.at[sub, pl.ds(part * step, step), :],
            sems.at[sub * PARTS + part],
        )
        for sub in range(z.subs)
        for part in range(PARTS)
    ]
    for copy in copies:
        copy.start()
    per = z.slots_per_lane
    base = per * z.loads
    for lane in range(LANES):
        for pos in range(per):
            face = tab[lane * per + pos]
            sub = face // z.faces
            start = pl.multiple_of((face - sub * z.faces) * z.dof, z.dof)
            row = base + pos * z.primal
            lanes[lane][row:row + z.primal, :] = coupling[sub, :, pl.ds(start, z.dof)]
        lanes[lane][base + per * z.primal:z.carry_rows, :] = corner_row[...]
    weights[...] = jnp.zeros_like(weights)
    gap = jnp.zeros((PAD - z.primal, z.unknowns), F32)
    for sub in range(z.subs):
        high, low = split_hi_lo(jnp.concatenate([coupling[sub], gap], axis=0))
        weights[sub, sub * 2 * PAD:sub * 2 * PAD + PAD, :] = high
        weights[sub, sub * 2 * PAD + PAD:sub * 2 * PAD + 2 * PAD, :] = low
    apply_in_kernel(z, load, [], weights, spot, near, copies, packed, image, small)
    for lane in range(LANES):
        for pos in range(per):
            lanes[lane][pos * z.loads:(pos + 1) * z.loads, :] = image[tab[lane * per + pos]]
    for lane in EARLY:
        for group in range(z.groups + 1):
            row = z.carry_rows + group * z.loads
            lanes[lane][row:row + z.loads, :] = small[group]


def precond_kernel(z, tab, weighted, residual, old_image, weights, spot, stiff, *rest):
    arrived, rest = rest[:LANES], rest[LANES:]
    vec, image, small = rest[:3]
    lanes, (packed, held) = rest[3:3 + LANES], rest[3 + LANES:]
    take_lanes(z, arrived, held)
    gamma = jnp.zeros((z.loads, z.dof), F32)
    eta = jnp.zeros((z.loads, z.dof), F32)
    for face in range(z.total):
        value = 0.25 * (weighted[face] - held[tab[z.slots + face]])
        vec[face] = value
        gamma = gamma + residual[face] * value
        eta = eta + old_image[face] * value
    apply_in_kernel(z, vec, [gamma, eta], weights, spot, stiff, None, packed, image, small)
    fill_lanes(z, tab, image, lanes)


def coarse_in_kernel(z, summed, inv_high, inv_low, pick, picked):
    n = z.loads
    primal = jnp.concatenate([summed[group] for group in range(z.groups)], axis=1)
    high, low = split_hi_lo(primal)
    both = jnp.dot(jnp.concatenate([high, low], axis=0), inv_high[...], preferred_element_type=F32)
    lifted = (both[0:n] + both[n:]) + jnp.dot(high, inv_low[...], preferred_element_type=F32)
    energy = jnp.sum(primal * lifted, axis=1, keepdims=True)
    high, low = split_hi_lo(lifted)
    values = jnp.dot(jnp.concatenate([high, low], axis=0), pick[...], preferred_element_type=F32)
    column = lax.broadcasted_iota(jnp.int32, (n, WIDE), 1)
    for block in range(z.blocks):
        group, place = divmod(block * PAD, WIDE)
        upper = values[0:n, group * WIDE:(group + 1) * WIDE]
        lower = values[n:, group * WIDE:(group + 1) * WIDE]
        first = pltpu.roll(upper, (WIDE - place) % WIDE, 1)
        second = pltpu.roll(upper, (WIDE + PAD - place) % WIDE, 1)
        third = pltpu.roll(lower, (WIDE + 2 * PAD - place) % WIDE, 1)
        mixed = jnp.where(column < PAD, first, jnp.where(column < 2 * PAD, second, third))
        picked[block] = jnp.where(column < 3 * PAD, mixed, 0.0).astype(BF)
    return energy


def image_of_face(z, tab, face, image, held, picked, spread):
    sides = jnp.concatenate([picked[face // z.faces], picked[tab[z.slots + z.total + face]]], axis=1)
    lift = jnp.dot(sides, spread[face], preferred_element_type=F32)
    return (image[face] - held[tab[z.slots + face]]) + lift


def start_kernel(z, tab, image, summed, upper, lower, pick, spread, blocks, *rest):
    arrived, rest = rest[:LANES], rest[LANES:]
    residual, weighted = rest[:2]
    lanes, (held, picked) = rest[2:2 + LANES], rest[2 + LANES:]
    for lane in range(LANES):
        for pos in range(z.slots_per_lane):
            held[lane * z.slots_per_lane + pos] = arrived[lane][pos * z.loads:(pos + 1) * z.loads, :]
    coarse_in_kernel(z, summed, upper, lower, pick, picked)
    for face in range(z.total):
        value = image_of_face(z, tab, face, image, held, picked, spread)
        residual[face] = value
        weighted[face] = jnp.dot(value.astype(BF), blocks[face], preferred_element_type=F32)
    fill_lanes(z, tab, weighted, lanes)


def step_kernel(first, last, z, tab, image, summed, upper, lower, pick, spread, blocks, vec, old_residual, *rest):
    if not first:
        old_solution, old_direction, old_image, old_scalars = rest[:4]
        rest = rest[4:]
    arrived, rest = rest[:LANES], rest[LANES:]
    solution_out, residual = rest[:2]
    rest = rest[2:]
    if not last:
        direction, new_image, scalars, weighted = rest[:4]
        lanes, rest = rest[4:4 + LANES], rest[4 + LANES:]
    held, picked = rest
    take_lanes(z, arrived, held)
    energy = coarse_in_kernel(z, summed, upper, lower, pick, picked)
    scalar = summed[z.groups]
    kappa, gamma, eta = [scalar[:, place:place + 1] for place in range(3)]
    curvature = 2.0 * (kappa + energy)
    beta = None
    if not first:
        beta = gamma / old_scalars[:, 0:1]
        curvature = curvature + beta * (2.0 * eta + beta * old_scalars[:, 1:2])
    alpha = gamma / curvature
    if not last:
        column = lax.broadcasted_iota(jnp.int32, (z.loads, WIDE), 1)
        scalars[...] = jnp.where(column == 0, gamma, curvature)
    wide = (z.loads, z.dof)
    alpha_wide = jnp.broadcast_to(alpha, wide)
    beta_wide = None if first else jnp.broadcast_to(beta, wide)
    for face in range(z.total):
        ahead = image_of_face(z, tab, face, image, held, picked, spread)
        along = vec[face]
        if not first:
            ahead = ahead + beta_wide * old_image[face]
            along = along + beta_wide * old_direction[face]
        moved = alpha_wide * along
        solution_out[face] = moved if first else old_solution[face] + moved
        value = old_residual[face] - alpha_wide * ahead
        residual[face] = value
        if not last:
            direction[face] = along
            new_image[face] = ahead
            weighted[face] = jnp.dot(value.astype(BF), blocks[face], preferred_element_type=F32)
    if not last:
        fill_lanes(z, tab, weighted, lanes)


def exchange(lanes, devices):
    return [lax.ppermute(lane, "sub", pairs) for lane, pairs in zip(lanes, lane_pairs(devices))]


def exchange_in_turn(lanes, devices):
    pairs = lane_pairs(devices)
    early = {lane: lax.ppermute(lanes[lane], "sub", pairs[lane]) for lane in EARLY}
    late = [lane for lane in range(LANES) if lane not in EARLY]
    near, waiting = lax.optimization_barrier(([early[0], early[1]], [lanes[lane] for lane in late]))
    early[0], early[1] = near
    early.update({lane: lax.ppermute(value, "sub", pairs[lane]) for lane, value in zip(late, waiting)})
    return [early[lane] for lane in range(LANES)]


def gathered(rows, devices):
    pair = jnp.concatenate([rows, lax.ppermute(rows, "sub", flipped(2, devices))])
    stacks = [(0, pair)] + [(mask, lax.ppermute(pair, "sub", flipped(mask, devices))) for mask in range(4, devices, 4)]
    return stacks + [(mask ^ 1, lax.ppermute(stack, "sub", flipped(1, devices))) for mask, stack in stacks]


def first_exchange(lanes, small, devices):
    pairs = lane_pairs(devices)
    arrived = {lane: lax.ppermute(lanes[lane], "sub", pairs[lane]) for lane in EARLY}
    across, crossed, beside = [
        lax.optimization_barrier(arrived[lane])[-small.size // WIDE:].reshape(small.shape) for lane in EARLY
    ]
    plane = (small + beside) + (across + crossed)
    late = [lane for lane in range(LANES) if lane not in EARLY]
    plane, waiting = lax.optimization_barrier((plane, [lanes[lane] for lane in late]))
    arrived.update({lane: lax.ppermute(value, "sub", pairs[lane]) for lane, value in zip(late, waiting)})
    parts = [plane] + [lax.ppermute(plane, "sub", flipped(mask, devices)) for mask in range(4, devices, 4)]
    while len(parts) > 1:
        parts = [first + second for first, second in zip(parts[0::2], parts[1::2])]
    return [arrived[lane] for lane in range(LANES)], parts[0]


def over_devices(value, devices):
    masks = []
    mask = 4
    while mask < devices:
        masks.append(mask)
        mask *= 2
    for mask in masks + [1, 2]:
        value = value + lax.ppermute(value, "sub", flipped(mask, devices))
    return value


def on_device(load, stiff_inv, face_blocks, coupling, coarse_inv, corners, partner):
    devices = lax.axis_size("sub")
    z = Sizes(load, coupling, coarse_inv, devices)
    stacks = gathered(coarse_inv, devices)
    masks = tuple(mask for mask, _ in stacks)
    stacks = [stack for _, stack in stacks]
    tab = routing(partner, z.slots_per_lane)

    numbers = jnp.pad(corners.astype(F32), ((0, 0), (0, PAD - z.primal)), constant_values=-1.0)
    row = jnp.pad(numbers.reshape(1, -1), ((0, 0), (0, WIDE - z.subs * PAD)), constant_values=-1.0)
    corner_row = jnp.broadcast_to(row, (8, WIDE))
    apart = jnp.pad(numbers, ((0, 0), (0, WIDE // z.subs - PAD)), constant_values=-1.0)
    spot = (apart.reshape(WIDE)[:, None] == jnp.arange(z.coarse, dtype=F32)[None, :]).astype(BF)

    field = shape(z.total, z.loads, z.dof)
    lane_field = [shape(z.slots_per_lane, z.loads, z.dof)] * LANES
    held = pltpu.VMEM((z.slots, z.loads, z.dof), F32)
    picked = pltpu.VMEM((z.blocks, z.loads, WIDE), BF)
    apply_scratch = [pltpu.VMEM((z.subs, 2 * z.loads, z.unknowns), BF)]
    apply_cost = dict(flops=2 * z.total * z.dof * z.unknowns * z.loads, moved=stiff_inv.size * 2)

    load_faces = load.reshape(z.total, z.loads, z.dof)
    small_shape = shape(z.groups + 1, z.loads, WIDE)
    image, small, *lanes = call(
        load_kernel, z,
        [field, small_shape]
        + [shape(z.carry_rows + (z.groups + 1) * z.loads * (lane in EARLY), z.dof) for lane in range(LANES)]
        + [shape(z.subs, z.unknowns, z.unknowns, dtype=BF), shape(z.subs, 4 * PAD, z.unknowns, dtype=BF)],
        (tab, load_faces, coupling, corner_row, spot, stiff_inv), [SMEM] + [VMEM] * 4 + [HBM],
        apply_scratch + [pltpu.SemaphoreType.DMA((z.subs * PARTS,))], FIRST_LIMIT, "apply_load", **apply_cost,
    )
    near, weights = lanes[LANES:]
    arrived, summed = first_exchange(lanes[:LANES], small, devices)
    spread, pick = call(
        unpack_kernel, z,
        [shape(z.total, 8 * PAD, z.dof, dtype=BF), shape(z.coarse, z.pick_width, dtype=BF)],
        (tab, coupling, corner_row, *arrived), [SMEM] + [VMEM] * (2 + LANES),
        [pltpu.VMEM((z.slots, z.primal, z.dof), F32), pltpu.VMEM((8, z.pick_width), F32)],
        8, "unpack_coupling",
    )
    blocks = face_blocks.reshape(z.total, z.dof, z.dof)
    inv_shape = shape(z.coarse, z.coarse, dtype=BF)
    upper, lower = call(
        functools.partial(assemble_kernel, masks), z, [inv_shape, inv_shape],
        (lax.axis_index("sub").reshape(1).astype(jnp.int32), *stacks),
        [SMEM] + [VMEM] * len(masks), [], 8, "assemble_coarse",
    )
    fixed = (upper, lower, pick, spread, blocks)
    residual, weighted, *lanes = call(
        start_kernel, z, [field, field] + lane_field,
        (tab, image, summed, *fixed, *arrived), [SMEM] + [VMEM] * (7 + LANES),
        [held, picked], 8, "first_residual",
    )
    state = None
    for iteration in range(ITERS):
        first, last = iteration == 0, iteration + 1 == ITERS
        arrived = exchange(lanes, devices)
        old_image = residual if first else state[2]
        vec, image, small, *lanes = call(
            precond_kernel, z, [field, field, small_shape] + lane_field,
            (tab, weighted, residual, old_image, weights, spot, near, *arrived),
            [SMEM] + [VMEM] * (6 + LANES),
            apply_scratch + [held], 8, "precond_apply", **apply_cost,
        )
        summed = over_devices(small, devices)
        arrived = exchange_in_turn(lanes, devices)
        ins = [tab, image, summed, *fixed, vec, residual] + ([] if first else list(state)) + list(arrived)
        outs = [field, field] + ([] if last else [field, field, shape(z.loads, WIDE), field] + lane_field)
        result = call(
            functools.partial(step_kernel, first, last), z, outs, ins, [SMEM] + [VMEM] * (len(ins) - 1),
            [held, picked], 8, "cg_step",
        )
        multipliers, residual = result[:2]
        if not last:
            direction, old, scalars, weighted = result[2:6]
            lanes = result[6:]
            state = (multipliers, direction, old, scalars)
    return multipliers.reshape(load.shape), residual.reshape(load.shape)


def solution(mesh):
    return jax.shard_map(
        on_device,
        mesh=mesh,
        in_specs=(
            P(("parts", "sub"), None, None, None),
            P(("parts", "sub"), None, None),
            P(("parts", "sub"), None, None, None),
            P(("parts", "sub"), None, None),
            P(("parts", "sub"), None),
            P(("parts", "sub"), None),
            P(("parts", "sub"), None),
        ),
        out_specs=(P(("parts", "sub"), None, None, None), P(("parts", "sub"), None, None, None)),
        check_vma=False,
    )
```

```python
import functools
import jax
import jax.numpy as jnp
from jax import lax
from jax.experimental import pallas as pl
from jax.experimental.pallas import tpu as pltpu
from jax.sharding import PartitionSpec as P

ITERS = 3
LANES = 6
EARLY = (0, 1, 5)
PAD = 32
WIDE = 128
BF = jnp.bfloat16
F32 = jnp.float32
VMEM = pl.BlockSpec(memory_space=pltpu.VMEM)
SMEM = pl.BlockSpec(memory_space=pltpu.SMEM)
HBM = pl.BlockSpec(memory_space=pltpu.HBM)
PARTS = 8
FIRST_LIMIT = 31
FIRST_FLOPS = 2 * 10**10
NT = (((1,), (1,)), ((), ()))


def matching(pairs, rest):
    both = list(pairs) + list(rest)
    return sorted(both + [(second, first) for first, second in both])


def flipped(mask, devices):
    return [(i, i ^ mask) for i in range(devices)]


def lane_pairs(devices):
    odd = range(2, devices - 2, 4)
    ends = [(0, 1), (devices - 2, devices - 1)]
    return (
        flipped(2, devices),
        flipped(3, devices),
        matching([(i + core, i + 2 + core) for i in odd for core in (0, 1)], ends),
        matching([(i + core, i + 3 - core) for i in odd for core in (0, 1)], ends),
        matching([(i, i + 3) for i in range(1, devices - 3, 2)], [(0, devices - 3), (2, devices - 1)]),
        flipped(1, devices),
    )


def split_hi_lo(value):
    high = value.astype(BF)
    return high, (value - high.astype(F32)).astype(BF)


def routing(partner, capacity):
    face_count = partner.size
    subs = partner.shape[0]
    own = lax.axis_index("sub")
    ids = partner.reshape(face_count)
    peer = ids // face_count
    chip_gap = jnp.abs(peer // 2 - own // 2)
    lowest = jnp.minimum(peer // 2, own // 2)
    crossed = (peer + own) % 2
    lane = jnp.where(chip_gap == 0, 5, jnp.where(chip_gap == 1, 2 * (lowest % 2) + crossed, 4))
    order = jnp.arange(face_count, dtype=jnp.int32)
    same = lane[:, None] == lane[None, :]
    send_pos = jnp.sum(same & (order[None, :] < order[:, None]), axis=1, dtype=jnp.int32)
    recv_pos = jnp.sum(same & (ids[None, :] < ids[:, None]), axis=1, dtype=jnp.int32)
    slots = jnp.arange(LANES * capacity, dtype=jnp.int32)
    hit = slots[:, None] == (lane * capacity + send_pos)[None, :]
    source = jnp.sum(jnp.where(hit, order[None, :], 0), axis=1, dtype=jnp.int32)
    arrival = lane * capacity + recv_pos
    block = (1 + lane) * subs + (ids // partner.shape[1]) % subs
    return jnp.concatenate([source, arrival, block]).astype(jnp.int32)


class Sizes:
    def __init__(self, load, coupling, coarse_inv, devices):
        self.subs, self.faces, self.loads, self.dof = load.shape
        self.total = self.subs * self.faces
        self.unknowns = self.faces * self.dof
        self.slots_per_lane = 3 * self.total // 8
        self.slots = LANES * self.slots_per_lane
        self.primal = coupling.shape[1]
        self.coarse = coarse_inv.shape[1]
        self.own_rows = coarse_inv.shape[0]
        self.groups = self.coarse // WIDE
        self.blocks = (1 + LANES) * self.subs
        self.pick_width = -(-self.blocks * PAD // WIDE) * WIDE
        self.carry_rows = self.slots_per_lane * (self.loads + self.primal) + 8


def call(kernel, sizes, outs, ins, specs, scratch, limit, name, flops=0, moved=0):
    return pl.pallas_call(
        functools.partial(kernel, sizes),
        out_shape=outs,
        in_specs=specs,
        out_specs=[VMEM] * len(outs),
        scratch_shapes=scratch,
        compiler_params=pltpu.CompilerParams(vmem_limit_bytes=limit * 2**20),
        cost_estimate=pl.CostEstimate(flops=flops, bytes_accessed=moved, transcendentals=0),
        name=name,
    )(*ins)


def shape(*dims, dtype=F32):
    return jax.ShapeDtypeStruct(dims, dtype)


def unpack_kernel(z, tab, coupling, corner_row, *rest):
    arrived, rest = rest[:LANES], rest[LANES:]
    spread, pick, held, names = rest
    per = z.slots_per_lane
    width = z.subs * PAD
    names[...] = jnp.full(names.shape, -1.0, F32)
    names[:, 0:width] = corner_row[:, 0:width]
    for lane in range(LANES):
        names[:, (1 + lane) * width:(2 + lane) * width] = arrived[lane][per * (z.loads + z.primal):per * (z.loads + z.primal) + 8, 0:width]
        for pos in range(per):
            row = per * z.loads + pos * z.primal
            held[lane * per + pos] = arrived[lane][row:row + z.primal, :]
    rows = lax.broadcasted_iota(jnp.int32, pick.shape, 0).astype(F32)
    pick[...] = jnp.where(rows == names[0:1, :], 1.0, 0.0).astype(BF)
    gap = jnp.zeros((PAD - z.primal, z.dof), F32)
    blank = jnp.zeros((PAD, z.dof), BF)
    for face in range(z.total):
        sub, side = face // z.faces, face % z.faces
        own = coupling[sub, :, side * z.dof:(side + 1) * z.dof]
        other = -held[tab[z.slots + face]]
        for place, value in enumerate((own, other)):
            high, low = split_hi_lo(jnp.concatenate([value, gap], axis=0))
            spread[face, place * 4 * PAD:(place + 1) * 4 * PAD, :] = jnp.concatenate([high, low, high, blank], axis=0)


def assemble_kernel(masks, z, own, *rest):
    stacks, (upper, lower) = rest[:len(masks)], rest[len(masks):]
    count = z.own_rows
    for mask, stack in zip(masks, stacks):
        for place, flip in enumerate((mask, mask ^ 2)):
            start = pl.multiple_of((own[0] ^ flip) * count, count)
            high, low = split_hi_lo(stack[place * count:(place + 1) * count, :])
            upper[pl.ds(start, count), :] = high
            lower[pl.ds(start, count), :] = low


def apply_in_kernel(z, vec, scalars, weights, spot, stiff, copies, packed, image, small):
    for face in range(z.total):
        sub, side = face // z.faces, face % z.faces
        high, low = split_hi_lo(vec[face])
        packed[sub, 0:z.loads, side * z.dof:(side + 1) * z.dof] = high
        packed[sub, z.loads:, side * z.dof:(side + 1) * z.dof] = low
    n = z.loads
    rows = jnp.zeros((2 * n, WIDE), F32)
    for sub in range(z.subs):
        rows = rows + lax.dot_general(packed[sub], weights[sub], NT, preferred_element_type=F32)
    rows = rows[0:n] + rows[n:]
    rows = rows + pltpu.roll(rows, WIDE - PAD, 1)
    column = lax.broadcasted_iota(jnp.int32, (n, WIDE), 1)
    rows = jnp.where(column % (2 * PAD) < PAD, rows, 0.0)
    summed = jnp.dot(jnp.concatenate(split_hi_lo(rows), axis=0), spot[...], preferred_element_type=F32)
    summed = summed[0:n] + summed[n:]
    for group in range(z.groups):
        small[group] = summed[:, group * WIDE:(group + 1) * WIDE]
    step = z.unknowns // PARTS
    kappa = jnp.zeros((n, z.dof), F32)
    for sub in range(z.subs):
        total = jnp.zeros((2 * n, z.unknowns), F32)
        for part in range(PARTS):
            if copies:
                copies[sub * PARTS + part].wait()
            total = total + jnp.dot(
                packed[sub, :, part * step:(part + 1) * step],
                stiff[sub, part * step:(part + 1) * step, :],
                preferred_element_type=F32,
            )
        total = total[0:n] + total[n:]
        for side in range(z.faces):
            piece = total[:, side * z.dof:(side + 1) * z.dof]
            image[sub * z.faces + side] = piece
            kappa = kappa + piece * vec[sub * z.faces + side]
    tail = jnp.zeros((n, WIDE), F32)
    for place, value in enumerate([kappa] + scalars):
        tail = jnp.where(column == place, jnp.sum(value, axis=1, keepdims=True), tail)
    small[z.groups] = tail


def fill_lanes(z, tab, field, lanes):
    for lane in range(LANES):
        for pos in range(z.slots_per_lane):
            lanes[lane][pos] = field[tab[lane * z.slots_per_lane + pos]]


def take_lanes(z, arrived, held):
    per = z.slots_per_lane
    for lane in range(LANES):
        held[lane * per:(lane + 1) * per] = arrived[lane][0:per]


def load_kernel(z, tab, load, coupling, corner_row, spot, stiff, image, small, *rest):
    lanes, (near, weights, packed, sems) = rest[:LANES], rest[LANES:]
    step = z.unknowns // PARTS
    copies = [
        pltpu.make_async_copy(
            stiff.at[sub, pl.ds(part * step, step), :],
            near.at[sub, pl.ds(part * step, step), :],
            sems.at[sub * PARTS + part],
        )
        for sub in range(z.subs)
        for part in range(PARTS)
    ]
    for copy in copies:
        copy.start()
    per = z.slots_per_lane
    base = per * z.loads
    for lane in range(LANES):
        for pos in range(per):
            face = tab[lane * per + pos]
            sub = face // z.faces
            start = pl.multiple_of((face - sub * z.faces) * z.dof, z.dof)
            row = base + pos * z.primal
            lanes[lane][row:row + z.primal, :] = coupling[sub, :, pl.ds(start, z.dof)]
        lanes[lane][base + per * z.primal:z.carry_rows, :] = corner_row[...]
    weights[...] = jnp.zeros_like(weights)
    gap = jnp.zeros((PAD - z.primal, z.unknowns), F32)
    for sub in range(z.subs):
        high, low = split_hi_lo(jnp.concatenate([coupling[sub], gap], axis=0))
        weights[sub, sub * 2 * PAD:sub * 2 * PAD + PAD, :] = high
        weights[sub, sub * 2 * PAD + PAD:sub * 2 * PAD + 2 * PAD, :] = low
    apply_in_kernel(z, load, [], weights, spot, near, copies, packed, image, small)
    for lane in range(LANES):
        for pos in range(per):
            lanes[lane][pos * z.loads:(pos + 1) * z.loads, :] = image[tab[lane * per + pos]]
    for lane in EARLY:
        for group in range(z.groups + 1):
            row = z.carry_rows + group * z.loads
            lanes[lane][row:row + z.loads, :] = small[group]


def precond_kernel(z, tab, weighted, residual, old_image, weights, spot, stiff, *rest):
    arrived, rest = rest[:LANES], rest[LANES:]
    vec, image, small = rest[:3]
    lanes, (packed, held) = rest[3:3 + LANES], rest[3 + LANES:]
    take_lanes(z, arrived, held)
    gamma = jnp.zeros((z.loads, z.dof), F32)
    eta = jnp.zeros((z.loads, z.dof), F32)
    for face in range(z.total):
        value = 0.25 * (weighted[face] - held[tab[z.slots + face]])
        vec[face] = value
        gamma = gamma + residual[face] * value
        eta = eta + old_image[face] * value
    apply_in_kernel(z, vec, [gamma, eta], weights, spot, stiff, None, packed, image, small)
    fill_lanes(z, tab, image, lanes)


def coarse_in_kernel(z, summed, inv_high, inv_low, pick, picked):
    n = z.loads
    primal = jnp.concatenate([summed[group] for group in range(z.groups)], axis=1)
    high, low = split_hi_lo(primal)
    both = jnp.dot(jnp.concatenate([high, low], axis=0), inv_high[...], preferred_element_type=F32)
    lifted = (both[0:n] + both[n:]) + jnp.dot(high, inv_low[...], preferred_element_type=F32)
    energy = jnp.sum(primal * lifted, axis=1, keepdims=True)
    high, low = split_hi_lo(lifted)
    values = jnp.dot(jnp.concatenate([high, low], axis=0), pick[...], preferred_element_type=F32)
    column = lax.broadcasted_iota(jnp.int32, (n, WIDE), 1)
    for block in range(z.blocks):
        group, place = divmod(block * PAD, WIDE)
        upper = values[0:n, group * WIDE:(group + 1) * WIDE]
        lower = values[n:, group * WIDE:(group + 1) * WIDE]
        first = pltpu.roll(upper, (WIDE - place) % WIDE, 1)
        second = pltpu.roll(upper, (WIDE + PAD - place) % WIDE, 1)
        third = pltpu.roll(lower, (WIDE + 2 * PAD - place) % WIDE, 1)
        mixed = jnp.where(column < PAD, first, jnp.where(column < 2 * PAD, second, third))
        picked[block] = jnp.where(column < 3 * PAD, mixed, 0.0).astype(BF)
    return energy


def image_of_face(z, tab, face, image, held, picked, spread):
    sides = jnp.concatenate([picked[face // z.faces], picked[tab[z.slots + z.total + face]]], axis=1)
    lift = jnp.dot(sides, spread[face], preferred_element_type=F32)
    return (image[face] - held[tab[z.slots + face]]) + lift


def start_kernel(z, tab, image, summed, upper, lower, pick, spread, blocks, *rest):
    arrived, rest = rest[:LANES], rest[LANES:]
    residual, weighted = rest[:2]
    lanes, (held, picked) = rest[2:2 + LANES], rest[2 + LANES:]
    for lane in range(LANES):
        for pos in range(z.slots_per_lane):
            held[lane * z.slots_per_lane + pos] = arrived[lane][pos * z.loads:(pos + 1) * z.loads, :]
    coarse_in_kernel(z, summed, upper, lower, pick, picked)
    for face in range(z.total):
        value = image_of_face(z, tab, face, image, held, picked, spread)
        residual[face] = value
        weighted[face] = jnp.dot(value.astype(BF), blocks[face], preferred_element_type=F32)
    fill_lanes(z, tab, weighted, lanes)


def step_kernel(first, last, z, tab, image, summed, upper, lower, pick, spread, blocks, vec, old_residual, *rest):
    if not first:
        old_solution, old_direction, old_image, old_scalars = rest[:4]
        rest = rest[4:]
    arrived, rest = rest[:LANES], rest[LANES:]
    solution_out, residual = rest[:2]
    rest = rest[2:]
    if not last:
        direction, new_image, scalars, weighted = rest[:4]
        lanes, rest = rest[4:4 + LANES], rest[4 + LANES:]
    held, picked = rest
    take_lanes(z, arrived, held)
    energy = coarse_in_kernel(z, summed, upper, lower, pick, picked)
    scalar = summed[z.groups]
    kappa, gamma, eta = [scalar[:, place:place + 1] for place in range(3)]
    curvature = 2.0 * (kappa + energy)
    beta = None
    if not first:
        beta = gamma / old_scalars[:, 0:1]
        curvature = curvature + beta * (2.0 * eta + beta * old_scalars[:, 1:2])
    alpha = gamma / curvature
    if not last:
        column = lax.broadcasted_iota(jnp.int32, (z.loads, WIDE), 1)
        scalars[...] = jnp.where(column == 0, gamma, curvature)
    wide = (z.loads, z.dof)
    alpha_wide = jnp.broadcast_to(alpha, wide)
    beta_wide = None if first else jnp.broadcast_to(beta, wide)
    for face in range(z.total):
        ahead = image_of_face(z, tab, face, image, held, picked, spread)
        along = vec[face]
        if not first:
            ahead = ahead + beta_wide * old_image[face]
            along = along + beta_wide * old_direction[face]
        moved = alpha_wide * along
        solution_out[face] = moved if first else old_solution[face] + moved
        value = old_residual[face] - alpha_wide * ahead
        residual[face] = value
        if not last:
            direction[face] = along
            new_image[face] = ahead
            weighted[face] = jnp.dot(value.astype(BF), blocks[face], preferred_element_type=F32)
    if not last:
        fill_lanes(z, tab, weighted, lanes)


def exchange(lanes, devices):
    return [lax.ppermute(lane, "sub", pairs) for lane, pairs in zip(lanes, lane_pairs(devices))]


def exchange_in_turn(lanes, devices):
    pairs = lane_pairs(devices)
    early = {lane: lax.ppermute(lanes[lane], "sub", pairs[lane]) for lane in EARLY}
    late = [lane for lane in range(LANES) if lane not in EARLY]
    near, waiting = lax.optimization_barrier(([early[0], early[1]], [lanes[lane] for lane in late]))
    early[0], early[1] = near
    early.update({lane: lax.ppermute(value, "sub", pairs[lane]) for lane, value in zip(late, waiting)})
    return [early[lane] for lane in range(LANES)]


def gathered(rows, devices):
    pair = jnp.concatenate([rows, lax.ppermute(rows, "sub", flipped(2, devices))])
    return [(0, pair)] + [(mask, lax.ppermute(pair, "sub", flipped(mask, devices))) for mask in range(4, devices, 4)]


def first_exchange(lanes, small, stacks, devices):
    arrived = exchange(lanes, devices)
    across, crossed, beside = [
        lax.optimization_barrier(arrived[lane])[-small.size // WIDE:].reshape(small.shape) for lane in EARLY
    ]
    plane = (small + beside) + (across + crossed)
    plane, stacks = lax.optimization_barrier((plane, stacks))
    stacks = stacks + [lax.ppermute(stack, "sub", flipped(1, devices)) for stack in stacks]
    parts = [plane] + [lax.ppermute(plane, "sub", flipped(mask, devices)) for mask in range(4, devices, 4)]
    while len(parts) > 1:
        parts = [first + second for first, second in zip(parts[0::2], parts[1::2])]
    return arrived, parts[0], stacks


def over_devices(value, devices):
    masks = []
    mask = 4
    while mask < devices:
        masks.append(mask)
        mask *= 2
    for mask in masks + [1, 2]:
        value = value + lax.ppermute(value, "sub", flipped(mask, devices))
    return value


def on_device(load, stiff_inv, face_blocks, coupling, coarse_inv, corners, partner):
    devices = lax.axis_size("sub")
    z = Sizes(load, coupling, coarse_inv, devices)
    stacks = gathered(coarse_inv, devices)
    masks = tuple(mask for mask, _ in stacks)
    masks = masks + tuple(mask ^ 1 for mask in masks)
    stacks = [stack for _, stack in stacks]
    coupling, stacks[0] = lax.optimization_barrier((coupling, stacks[0]))
    tab = routing(partner, z.slots_per_lane)

    numbers = jnp.pad(corners.astype(F32), ((0, 0), (0, PAD - z.primal)), constant_values=-1.0)
    row = jnp.pad(numbers.reshape(1, -1), ((0, 0), (0, WIDE - z.subs * PAD)), constant_values=-1.0)
    corner_row = jnp.broadcast_to(row, (8, WIDE))
    apart = jnp.pad(numbers, ((0, 0), (0, WIDE // z.subs - PAD)), constant_values=-1.0)
    spot = (apart.reshape(WIDE)[:, None] == jnp.arange(z.coarse, dtype=F32)[None, :]).astype(BF)

    field = shape(z.total, z.loads, z.dof)
    lane_field = [shape(z.slots_per_lane, z.loads, z.dof)] * LANES
    held = pltpu.VMEM((z.slots, z.loads, z.dof), F32)
    picked = pltpu.VMEM((z.blocks, z.loads, WIDE), BF)
    apply_scratch = [pltpu.VMEM((z.subs, 2 * z.loads, z.unknowns), BF)]
    apply_cost = dict(flops=2 * z.total * z.dof * z.unknowns * z.loads, moved=stiff_inv.size * 2)

    load_faces = load.reshape(z.total, z.loads, z.dof)
    small_shape = shape(z.groups + 1, z.loads, WIDE)
    image, small, *lanes = call(
        load_kernel, z,
        [field, small_shape]
        + [shape(z.carry_rows + (z.groups + 1) * z.loads * (lane in EARLY), z.dof) for lane in range(LANES)]
        + [shape(z.subs, z.unknowns, z.unknowns, dtype=BF), shape(z.subs, 4 * PAD, z.unknowns, dtype=BF)],
        (tab, load_faces, coupling, corner_row, spot, stiff_inv), [SMEM] + [VMEM] * 4 + [HBM],
        apply_scratch + [pltpu.SemaphoreType.DMA((z.subs * PARTS,))], FIRST_LIMIT, "apply_load", flops=FIRST_FLOPS, moved=stiff_inv.size * 2,
    )
    near, weights = lanes[LANES:]
    lanes, stacks = lax.optimization_barrier((lanes[:LANES], stacks))
    arrived, summed, stacks = first_exchange(lanes, small, stacks, devices)
    spread, pick = call(
        unpack_kernel, z,
        [shape(z.total, 8 * PAD, z.dof, dtype=BF), shape(z.coarse, z.pick_width, dtype=BF)],
        (tab, coupling, corner_row, *arrived), [SMEM] + [VMEM] * (2 + LANES),
        [pltpu.VMEM((z.slots, z.primal, z.dof), F32), pltpu.VMEM((8, z.pick_width), F32)],
        8, "unpack_coupling",
    )
    blocks = face_blocks.reshape(z.total, z.dof, z.dof)
    inv_shape = shape(z.coarse, z.coarse, dtype=BF)
    upper, lower = call(
        functools.partial(assemble_kernel, masks), z, [inv_shape, inv_shape],
        (lax.axis_index("sub").reshape(1).astype(jnp.int32), *stacks),
        [SMEM] + [VMEM] * len(masks), [], 8, "assemble_coarse",
    )
    fixed = (upper, lower, pick, spread, blocks)
    residual, weighted, *lanes = call(
        start_kernel, z, [field, field] + lane_field,
        (tab, image, summed, *fixed, *arrived), [SMEM] + [VMEM] * (7 + LANES),
        [held, picked], 8, "first_residual",
    )
    state = None
    for iteration in range(ITERS):
        first, last = iteration == 0, iteration + 1 == ITERS
        arrived = exchange(lanes, devices)
        old_image = residual if first else state[2]
        vec, image, small, *lanes = call(
            precond_kernel, z, [field, field, small_shape] + lane_field,
            (tab, weighted, residual, old_image, weights, spot, near, *arrived),
            [SMEM] + [VMEM] * (6 + LANES),
            apply_scratch + [held], 8, "precond_apply", **apply_cost,
        )
        summed = over_devices(small, devices)
        arrived = exchange_in_turn(lanes, devices)
        ins = [tab, image, summed, *fixed, vec, residual] + ([] if first else list(state)) + list(arrived)
        outs = [field, field] + ([] if last else [field, field, shape(z.loads, WIDE), field] + lane_field)
        result = call(
            functools.partial(step_kernel, first, last), z, outs, ins, [SMEM] + [VMEM] * (len(ins) - 1),
            [held, picked], 8, "cg_step",
        )
        multipliers, residual = result[:2]
        if not last:
            direction, old, scalars, weighted = result[2:6]
            lanes = result[6:]
            state = (multipliers, direction, old, scalars)
    return multipliers.reshape(load.shape), residual.reshape(load.shape)


def solution(mesh):
    return jax.shard_map(
        on_device,
        mesh=mesh,
        in_specs=(
            P(("parts", "sub"), None, None, None),
            P(("parts", "sub"), None, None),
            P(("parts", "sub"), None, None, None),
            P(("parts", "sub"), None, None),
            P(("parts", "sub"), None),
            P(("parts", "sub"), None),
            P(("parts", "sub"), None),
        ),
        out_specs=(P(("parts", "sub"), None, None, None), P(("parts", "sub"), None, None, None)),
        check_vma=False,
    )
```
